512 devices in a mesh: section: 16 (over y, core), dp: 32 (over z, x).
Axes of the slice: x: 4, y: 8, z: 8, core: 2. Of those that a mesh axis runs over, the one named last changes fastest.
Arguments:
- images: bfloat16 [2, 4096, 256], P(None, 'dp'), may hold values from -6 to 6
- cotangent: bfloat16 [2, 4096, 256], P(None, 'dp'), may hold values from -6 to 6
- w_in: bfloat16 [16, 2, 256, 256], P('section'), may hold values from -0.375 to 0.375
- w_out: bfloat16 [16, 2, 256, 256], P('section'), may hold values from -0.375 to 0.375
- gains: float32 [16, 2, 256], P('section'), may hold values from 0.1 to 1.9
- layer_counts: int32 [16], P('section'), may hold values from 1 to 2
Outputs:
- section_outputs: bfloat16 [16, 2, 4096, 256], P('section', None, 'dp')
- grad_in: float32 [16, 2, 256, 256], P('section', None, 'dp')
- grad_out: float32 [16, 2, 256, 256], P('section', None, 'dp')
- grad_gain: float32 [16, 2, 256], P('section', None, 'dp')
The draws below stay inside these ranges and needn't reach their ends.
All inputs are finite; a program needn't handle non-finite values.
Results may differ from the reference program's by a relative error of at most 0.04.
Values may be sent and summed in bfloat16 or wider, within the bound.
No kernel may reach another device: no remote copies, remote signals or barrier semaphores. Data moves between devices by JAX's collectives and lax.ppermute only.
A program may use at most 64 MiB of HBM per device.

```python
import jax
import jax.numpy as jnp
from jax import lax

C = 256
LAYERS = 2
MICRO = 2
PIX_DEV = 128
SECTIONS = 16
PIXELS = 4096
N_DP = 32


def plant(drawn, own_key, low, high):
    spot = [jax.random.randint(jax.random.fold_in(own_key, axis), (), 0, length) for axis, length in enumerate(drawn.shape)]
    widest = drawn.shape.index(max(drawn.shape))
    neighbour = spot[:widest] + [(spot[widest] + 1) % drawn.shape[widest]] + spot[widest + 1:]
    return drawn.at[tuple(spot)].set(low).at[tuple(neighbour)].set(high)


def shard_levels(stream_key, shape, shards, smallest, top_value):
    gain = 1.0
    for position, shards_of in shards:
        draws = jax.random.uniform(jax.random.fold_in(jax.random.fold_in(stream_key, 6), position), (shards_of,), jnp.float32, smallest / len(shards), top_value / len(shards))
        gain = gain * jnp.repeat(jnp.exp(draws), shape[position] // shards_of).reshape((-1,) + (1,) * (len(shape) - 1 - position))
    return gain


def normal_values(key, extent, spread, bound, split=(), held_as=jnp.bfloat16):
    array = spread * jax.random.normal(key, extent, jnp.float32)
    if split:
        array = array * shard_levels(key, extent, split, -0.22, 0.18)
    return jnp.clip(array, -bound, bound).astype(held_as)


def setup_inputs(seed: int = 0) -> dict:
    arg_keys = jax.random.split(jax.random.key(seed), 7)
    return {
        "images": normal_values(arg_keys[0], (MICRO, PIXELS, C), 1.0, 6.0, ((1, 32),)),
        "cotangent": normal_values(arg_keys[1], (MICRO, PIXELS, C), 1.0, 6.0, ((1, 32),)),
        "w_in": normal_values(arg_keys[2], (SECTIONS, LAYERS, C, C), C ** -0.5, 0.375, ((0, 16),)),
        "w_out": normal_values(arg_keys[3], (SECTIONS, LAYERS, C, C), C ** -0.5, 0.375, ((0, 16),)),
        "gains": jnp.clip(1.0 + 0.18 * jax.random.normal(arg_keys[4], (SECTIONS, LAYERS, C), jnp.float32), 0.1, 1.9),
        "layer_counts": plant(jax.random.randint(arg_keys[5], (SECTIONS,), 1, LAYERS + 1), jax.random.fold_in(arg_keys[5], 1), 1, LAYERS).astype(jnp.int32),
    }


def residual_block(inflow, first_w, second_w, gain_rows, active_layers):
    state = inflow
    for layer_index in range(first_w.shape[0]):
        mean_square = lax.optimization_barrier(jnp.mean(state * state, axis=-1, keepdims=True))
        normed = (state * lax.rsqrt(mean_square + 1e-06) * gain_rows[layer_index]).astype(jnp.bfloat16)
        pre_act = jnp.dot(normed, first_w[layer_index], preferred_element_type=jnp.float32)
        activation = jax.nn.silu(pre_act).astype(jnp.bfloat16)
        updated = state + jnp.dot(activation, second_w[layer_index], preferred_element_type=jnp.float32)
        state = jnp.where(layer_index < active_layers, updated, state)
    return state

def block_grads(inflow, upstream, first_w, second_w, gain_rows, active_layers):

    def local_block(inflow_value, first_value, second_value, gain_value):
        return residual_block(inflow_value, first_value, second_value, gain_value, active_layers)
    result, pull_back = jax.vjp(local_block, inflow, first_w, second_w, gain_rows)
    return pull_back(upstream)

def reference(images, cotangent, w_in, w_out, gains, layer_counts):
    sections = w_in.shape[0]
    half_sections = sections // 2
    channels = images.shape[2]
    outputs_all = []
    inflows_all = []
    for micro_index in range(MICRO):
        outflows = []
        inflows = []
        for section_index in range(sections):
            previous = images[micro_index] if section_index == 0 else outflows[section_index - 1]
            inflow = previous.astype(jnp.float32)
            if section_index >= half_sections:
                inflow = inflow + outflows[sections - 1 - section_index].astype(jnp.float32)
            inflows.append(inflow)
            outflows.append(residual_block(inflow, w_in[section_index], w_out[section_index], gains[section_index], layer_counts[section_index]).astype(jnp.bfloat16))
        outputs_all.append(outflows)
        inflows_all.append(inflows)
    section_outputs = jnp.stack([jnp.stack([outputs_all[m_index][s_index] for m_index in range(MICRO)]) for s_index in range(sections)])
    acc_in = [jnp.zeros(w_in.shape[1:], jnp.float32) for s_index in range(sections)]
    acc_out = [jnp.zeros(w_out.shape[1:], jnp.float32) for s_index in range(sections)]
    acc_gain = [jnp.zeros(gains.shape[1:], jnp.float32) for s_index in range(sections)]
    blockwise = jax.vmap(block_grads, in_axes=(0, 0, None, None, None, None))
    for micro_index in range(MICRO):
        sent = [None] * sections
        for section_index in range(sections - 1, -1, -1):
            if section_index == sections - 1:
                upstream = cotangent[micro_index].astype(jnp.float32)
            else:
                upstream = sent[section_index + 1].astype(jnp.float32)
                if section_index < half_sections:
                    upstream = upstream + sent[sections - 1 - section_index].astype(jnp.float32)
            inflow_blocks = inflows_all[micro_index][section_index].reshape(N_DP, PIX_DEV, channels)
            upstream_blocks = upstream.reshape(N_DP, PIX_DEV, channels)
            grad_parts = blockwise(inflow_blocks, upstream_blocks, w_in[section_index], w_out[section_index], gains[section_index], layer_counts[section_index])
            sent[section_index] = grad_parts[0].reshape(N_DP * PIX_DEV, channels).astype(jnp.bfloat16)
            acc_in[section_index] = acc_in[section_index] + lax.optimization_barrier(jnp.sum(grad_parts[1].astype(jnp.float32), axis=0))
            acc_out[section_index] = acc_out[section_index] + lax.optimization_barrier(jnp.sum(grad_parts[2].astype(jnp.float32), axis=0))
            acc_gain[section_index] = acc_gain[section_index] + lax.optimization_barrier(jnp.sum(grad_parts[3].astype(jnp.float32), axis=0))
    return (section_outputs, jnp.stack(acc_in), jnp.stack(acc_out), jnp.stack(acc_gain))
```

```python
import functools
import jax
import jax.numpy as jnp
from jax import lax
from jax.experimental import pallas as pl
from jax.experimental.pallas import tpu as pltpu
from jax.sharding import PartitionSpec as P

C = 256
EPS = 1e-06
F32 = jnp.float32
BF16 = jnp.bfloat16


def dot(a, b):
    return jnp.dot(a, b, preferred_element_type=F32)


def dot_t(a, b):
    return lax.dot_general(a, b, (((1,), (1,)), ((), ())), preferred_element_type=F32)


def dot_rows(a, b):
    return lax.dot_general(a, b, (((0,), (0,)), ((), ())), preferred_element_type=F32)


def scale_of(state):
    return lax.rsqrt(jnp.mean(state * state, axis=-1, keepdims=True) + EPS)


def layer_forward(state, gain, first, second):
    normed = (state * scale_of(state) * gain).astype(BF16)
    pre = dot(normed, first)
    act = (pre * jax.nn.sigmoid(pre)).astype(BF16)
    return state + dot(act, second), pre


def layer_backward(grad, state, pre, gain, first, second):
    d_act = dot_t(grad.astype(BF16), second)
    sig = jax.nn.sigmoid(pre)
    slope = sig * (1.0 + pre * (1.0 - sig))
    d_pre = (d_act * slope).astype(BF16)
    d_normed = dot_t(d_pre, first)
    scale = scale_of(state)
    unit = state * scale
    d_unit = d_normed * gain
    inner = jnp.mean(d_unit * unit, axis=-1, keepdims=True)
    return grad + scale * (d_unit - unit * inner)


def weight_copy(w_hbm, w_vmem, sems, section):
    return pltpu.make_async_copy(w_hbm.at[section], w_vmem.at[section], sems.at[section])


def forward_kernel(sections, counts, x_ref, g_ref, w_hbm, out_ref, inflow_ref, state_ref, pre_ref, w_vmem, sems):
    for s in range(sections):
        weight_copy(w_hbm, w_vmem, sems, s).start()
    half = sections // 2
    for s in range(sections):
        weight_copy(w_hbm, w_vmem, sems, s).wait()
        state = (x_ref[...] if s == 0 else out_ref[s - 1]).astype(F32)
        if s >= half:
            state = state + out_ref[sections - 1 - s].astype(F32)
        inflow_ref[s] = state.astype(BF16)
        state_ref[s, 0] = state
        state, pre = layer_forward(state, g_ref[s, 0][None], w_vmem[s, 0], w_vmem[s, 2])
        pre_ref[s, 0] = pre
        out_ref[s] = state.astype(BF16)

        @pl.when(counts[s] > 1)
        def _():
            state_ref[s, 1] = state
            after, pre = layer_forward(state, g_ref[s, 1][None], w_vmem[s, 1], w_vmem[s, 3])
            pre_ref[s, 1] = pre
            out_ref[s] = after.astype(BF16)


def backward_kernel(sections, counts, ct_ref, g_ref, state_ref, pre_ref, w_hbm, up_ref, w_vmem, sent_ref, grad_ref, sems):
    for s in reversed(range(sections)):
        weight_copy(w_hbm, w_vmem, sems, s).start()
    half = sections // 2
    for s in reversed(range(sections)):
        weight_copy(w_hbm, w_vmem, sems, s).wait()
        grad = (ct_ref[...] if s == sections - 1 else sent_ref[s + 1]).astype(F32)
        if s < half:
            grad = grad + sent_ref[sections - 1 - s].astype(F32)
        up_ref[s] = grad.astype(BF16)
        grad_ref[...] = grad

        @pl.when(counts[s] > 1)
        def _():
            grad_ref[...] = layer_backward(
                grad, state_ref[s, 1], pre_ref[s, 1], g_ref[s, 1][None], w_vmem[s, 1], w_vmem[s, 3]
            )

        grad = layer_backward(
            grad_ref[...], state_ref[s, 0], pre_ref[s, 0], g_ref[s, 0][None], w_vmem[s, 0], w_vmem[s, 2]
        )
        sent_ref[s] = grad.astype(BF16)


def owner_kernel(counts, inflow_ref, up_ref, g_ref, w_in_ref, w_out_ref, parts_ref, grad_ref, gw_ref):
    inflow = inflow_ref[...].astype(F32)
    after, pre0 = layer_forward(inflow, g_ref[0][None], w_in_ref[0], w_out_ref[0])
    grad_ref[...] = up_ref[...].astype(F32)

    def gradients(layer, state, pre, grad):
        gain = g_ref[layer][None]
        grad_cast = grad.astype(BF16)
        d_act = dot_t(grad_cast, w_out_ref[layer])
        sig = jax.nn.sigmoid(pre)
        act = (pre * sig).astype(BF16)
        d_pre = (d_act * (sig * (1.0 + pre * (1.0 - sig)))).astype(BF16)
        d_normed = dot_t(d_pre, w_in_ref[layer])
        scale = scale_of(state)
        unit = state * scale
        normed = (unit * gain).astype(BF16)
        gw_ref[layer] = dot_rows(normed, d_pre)
        gw_ref[2 + layer] = dot_rows(act, grad_cast)
        return scale, unit, d_normed * gain

    @pl.when(counts[0] > 1)
    def _():
        grad = grad_ref[...]
        pre1 = dot((after * scale_of(after) * g_ref[1][None]).astype(BF16), w_in_ref[1])
        scale, unit, d_unit = gradients(1, after, pre1, grad)
        inner = jnp.mean(d_unit * unit, axis=-1, keepdims=True)
        grad_ref[...] = grad + scale * (d_unit - unit * inner)

    @pl.when(counts[0] <= 1)
    def _():
        gw_ref[1] = jnp.zeros((C, C), F32)
        gw_ref[3] = jnp.zeros((C, C), F32)

    gradients(0, inflow, pre0, grad_ref[...])

    columns, _, _ = parts_ref.shape
    share = C // columns
    for matrix in range(2):
        both = [gw_ref[2 * matrix + layer].reshape(columns, share, C) for layer in range(2)]
        parts_ref[:, :, matrix * C : (matrix + 1) * C] = jnp.concatenate(both, 1).astype(BF16)


def sum_kernel(parts_ref, w_ref, g_ref, gw_in_ref, gw_out_ref, gain_ref):
    columns, double, _ = parts_ref.shape
    total = parts_ref[0].astype(F32)
    for source in range(1, columns):
        total = total + parts_ref[source].astype(F32)
    share = double // 2
    for layer in range(2):
        rows = total[layer * share : (layer + 1) * share]
        gw_in_ref[layer] = rows[:, :C]
        gw_out_ref[layer] = rows[:, C:]
        product = jnp.sum(rows[:, :C] * w_ref[layer], axis=1, keepdims=True)
        gain_ref[layer] = product / g_ref[layer]


def vmem():
    return pl.BlockSpec(memory_space=pltpu.VMEM)


def smem():
    return pl.BlockSpec(memory_space=pltpu.SMEM)


def hbm():
    return pl.BlockSpec(memory_space=pl.ANY)


def run_forward(counts, x, gains, weights):
    sections = weights.shape[0]
    rows = x.shape[0]
    shape = jax.ShapeDtypeStruct
    return pl.pallas_call(
        functools.partial(forward_kernel, sections),
        out_shape=(
            shape((sections, rows, C), BF16),
            shape((sections, rows, C), BF16),
            shape((sections, 2, rows, C), F32),
            shape((sections, 2, rows, C), F32),
        ),
        in_specs=[smem(), vmem(), vmem(), hbm()],
        out_specs=(vmem(),) * 4,
        scratch_shapes=[pltpu.VMEM(weights.shape, BF16), pltpu.SemaphoreType.DMA((sections,))],
        compiler_params=pltpu.CompilerParams(vmem_limit_bytes=48 * 2**20),
        name="chain_forward",
    )(counts, x, gains, weights)


def run_backward(counts, ct, gains, states, pres, weights):
    sections = weights.shape[0]
    rows = ct.shape[0]
    return pl.pallas_call(
        functools.partial(backward_kernel, sections),
        out_shape=jax.ShapeDtypeStruct((sections, rows, C), BF16),
        in_specs=[smem(), vmem(), vmem(), vmem(), vmem(), hbm()],
        out_specs=vmem(),
        scratch_shapes=[
            pltpu.VMEM(weights.shape, BF16),
            pltpu.VMEM((sections, rows, C), BF16),
            pltpu.VMEM((rows, C), F32),
            pltpu.SemaphoreType.DMA((sections,)),
        ],
        compiler_params=pltpu.CompilerParams(vmem_limit_bytes=48 * 2**20),
        cost_estimate=pl.CostEstimate(flops=4 * 10**9, bytes_accessed=9 * 2**20, transcendentals=10**6),
        name="chain_backward",
    )(counts, ct, gains, states, pres, weights)


def run_owner(counts, inflow, up, gains, w_in, w_out, columns):
    rows = inflow.shape[0]
    return pl.pallas_call(
        owner_kernel,
        out_shape=jax.ShapeDtypeStruct((columns, 2 * C // columns, 2 * C), BF16),
        in_specs=[smem()] + [vmem()] * 5,
        out_specs=vmem(),
        scratch_shapes=[pltpu.VMEM((rows, C), F32), pltpu.VMEM((4, C, C), F32)],
        compiler_params=pltpu.CompilerParams(vmem_limit_bytes=32 * 2**20),
        name="owner_gradients",
    )(counts, inflow, up, gains, w_in, w_out)


def run_sum(parts, w_rows, gain_rows):
    share = C // parts.shape[0]
    shape = jax.ShapeDtypeStruct
    return pl.pallas_call(
        sum_kernel,
        out_shape=(shape((2, share, C), F32), shape((2, share, C), F32), shape((2, share, 1), F32)),
        in_specs=[vmem()] * 3,
        out_specs=(vmem(),) * 3,
        compiler_params=pltpu.CompilerParams(vmem_limit_bytes=16 * 2**20),
        name="sum_parts",
    )(parts, w_rows, gain_rows)


def body(images, cotangent, w_in, w_out, gains, layer_counts):
    sections = lax.axis_size("section")
    columns = lax.axis_size("dp")
    here = lax.axis_index("section")
    micro, pixels, _ = images.shape
    rows = micro * pixels // sections

    weights = lax.all_gather(jnp.concatenate([w_in[0], w_out[0]]), "section", axis=0)
    small = jnp.concatenate([gains[0], jnp.broadcast_to(layer_counts.astype(F32)[:, None], (1, C))])
    small = jnp.broadcast_to(small[None], (sections, 3, C))
    small = lax.all_to_all(small, "section", 0, 0, tiled=True)
    all_gains = small[:, :2]
    all_counts = small[:, 2, 0].astype(jnp.int32)

    def own_rows(x):
        return lax.dynamic_index_in_dim(x.reshape(sections, rows, C), here, 0, keepdims=False)

    outs, inflows, states, pres = run_forward(all_counts, own_rows(images), all_gains, weights)
    there = lax.all_to_all(jnp.concatenate([outs, inflows], 1), "section", 0, 0, tiled=True)
    ups = run_backward(all_counts, own_rows(cotangent), all_gains, states, pres, weights)
    section_outputs = there[:, :rows].reshape(micro, pixels, C)
    inflow = there[:, rows:].reshape(micro * pixels, C)
    up = lax.all_to_all(ups, "section", 0, 0, tiled=True).reshape(micro * pixels, C)

    parts = run_owner(layer_counts, inflow, up, gains[0], w_in[0], w_out[0], columns)
    parts = lax.all_to_all(parts, "dp", 0, 0, tiled=True)
    share = C // columns
    start = lax.axis_index("dp") * share
    w_rows = lax.dynamic_slice_in_dim(w_in[0], start, share, 1).astype(F32)
    gain_rows = lax.dynamic_slice_in_dim(gains[0], start, share, 1)[:, :, None]
    grad_in, grad_out, grad_gain = run_sum(parts, w_rows, gain_rows)
    return section_outputs[None], grad_in[None], grad_out[None], grad_gain[None, :, :, 0]


def solution(mesh):
    return jax.shard_map(
        body,
        mesh=mesh,
        in_specs=(
            P(None, "dp", None),
            P(None, "dp", None),
            P("section", None, None, None),
            P("section", None, None, None),
            P("section", None, None),
            P("section"),
        ),
        out_specs=(
            P("section", None, "dp", None),
            P("section", None, "dp", None),
            P("section", None, "dp", None),
            P("section", None, "dp"),
        ),
        check_vma=False,
    )
```

```python
import jax
import jax.numpy as jnp
from jax import lax
from jax.experimental import pallas as pl
from jax.experimental.pallas import tpu as pltpu
from jax.sharding import PartitionSpec as P

C = 256
EPS = 1e-06
F32 = jnp.float32
BF16 = jnp.bfloat16
PACK = 4 * C + 16
FIRST, SECOND, MIDDLE, LAST = 0, 1, 3, 6


def dot(a, b):
    return jnp.dot(a, b, preferred_element_type=F32)


def dot_t(a, b):
    return lax.dot_general(a, b, (((1,), (1,)), ((), ())), preferred_element_type=F32)


def dot_rows(a, b):
    return lax.dot_general(a, b, (((0,), (0,)), ((), ())), preferred_element_type=F32)


def scale_of(state):
    return lax.rsqrt(jnp.mean(state * state, axis=-1, keepdims=True) + EPS)


def layer_forward(state, gain, first, second):
    normed = (state * scale_of(state) * gain).astype(BF16)
    pre = dot(normed, first)
    act = (pre * jax.nn.sigmoid(pre)).astype(BF16)
    return state + dot(act, second), pre


def layer_backward(grad, state, pre, gain, first, second):
    d_act = dot_t(grad.astype(BF16), second)
    sig = jax.nn.sigmoid(pre)
    slope = sig * (1.0 + pre * (1.0 - sig))
    d_pre = (d_act * slope).astype(BF16)
    d_normed = dot_t(d_pre, first)
    scale = scale_of(state)
    unit = state * scale
    d_unit = d_normed * gain
    inner = jnp.mean(d_unit * unit, axis=-1, keepdims=True)
    return grad + scale * (d_unit - unit * inner)


def position():
    here = lax.axis_index("section")
    return here // 2, here % 2


class Weights:
    def __init__(self, core, refs, packed, sems):
        self.refs, self.packed, self.sems, self.core = refs, packed, sems, core

    def copy(self, ref, slot):
        return pltpu.make_async_copy(ref, self.packed.at[slot], self.sems.at[slot])

    def start(self, pair):
        same, other = self.refs[2 * pair], self.refs[2 * pair + 1]
        self.copy(same, 2 * pair + self.core).start()
        self.copy(other, 2 * pair + 1 - self.core).start()

    def wait(self, slot):
        self.copy(self.refs[0], slot).wait()

    def tail(self, slot):
        return self.packed[slot, 4 * C :].astype(F32)

    def gain(self, slot, layer):
        tail = self.tail(slot)
        return tail[layer : layer + 1] + tail[2 + layer : 3 + layer] + tail[4 + layer : 5 + layer]

    def first(self, slot, layer):
        return self.packed[slot, layer * C : (layer + 1) * C]

    def second(self, slot, layer):
        return self.packed[slot, (2 + layer) * C : (3 + layer) * C]

    def both(self, slot):
        return jnp.max(self.tail(slot)[8:9]) > 1.5

    def forward(self, slot, state, state_ref, pre_ref, out_ref):
        state_ref[slot, 0] = state
        state, pre = layer_forward(state, self.gain(slot, 0), self.first(slot, 0), self.second(slot, 0))
        pre_ref[slot, 0] = pre
        out_ref[slot] = state.astype(BF16)

        @pl.when(self.both(slot))
        def _():
            state_ref[slot, 1] = state
            after, pre = layer_forward(state, self.gain(slot, 1), self.first(slot, 1), self.second(slot, 1))
            pre_ref[slot, 1] = pre
            out_ref[slot] = after.astype(BF16)

    def backward(self, slot, grad, state_ref, pre_ref, grad_ref):
        grad_ref[...] = grad

        def layer(number):
            return layer_backward(
                grad_ref[...],
                state_ref[slot, number],
                pre_ref[slot, number],
                self.gain(slot, number),
                self.first(slot, number),
                self.second(slot, number),
            )

        @pl.when(self.both(slot))
        def _():
            grad_ref[...] = layer(1)

        return layer(0).astype(BF16)


def pack_kernel(counts, w_in_ref, w_out_ref, g_ref, packed_ref):
    for layer in range(2):
        packed_ref[layer * C : (layer + 1) * C] = w_in_ref[layer]
        packed_ref[(2 + layer) * C : (3 + layer) * C] = w_out_ref[layer]
    gains = g_ref[...]
    coarse = gains.astype(BF16).astype(F32)
    rest = gains - coarse
    fine = rest.astype(BF16).astype(F32)
    count = jnp.full((2, C), counts[0].astype(F32))
    rows = [coarse, fine, rest - fine, jnp.zeros_like(coarse), count, jnp.zeros((6, C), F32)]
    packed_ref[4 * C :] = jnp.concatenate(rows, 0).astype(BF16)


def pair_kernel(chip, x_ref, same, other, outs_ref, last_ref, packed, states, pres, sems):
    here, core = position()

    @pl.when(here == chip)
    def _():
        weights = Weights(core, [same, other], packed, sems)
        weights.start(0)
        state = x_ref[...].astype(F32)
        for slot in range(2):
            weights.wait(slot)
            weights.forward(slot, state, states, pres, outs_ref)
            state = outs_ref[slot].astype(F32)
        last_ref[...] = outs_ref[1]


def middle_forward_kernel(x_ref, hop_ref, *refs):
    refs, (outs_ref, inflow_ref, hop_out, state_ref, pre_ref, packed, sems) = refs[:6], refs[6:]
    here, core = position()

    @pl.when((here == SECOND) | (here == MIDDLE))
    def _():
        weights = Weights(core, refs, packed, sems)
        for pair in range(3):
            weights.start(pair)
        for slot in range(6):
            weights.wait(slot)
            if slot == 0:
                state = jnp.where(here == SECOND, x_ref[...].astype(F32), hop_ref[...].astype(F32))
            else:
                state = outs_ref[slot - 1].astype(F32)
            if slot >= 4:
                state = state + outs_ref[7 - slot].astype(F32)
            inflow_ref[slot] = state.astype(BF16)
            weights.forward(slot, state, state_ref, pre_ref, outs_ref)
        hop_out[0] = outs_ref[5]
        hop_out[1] = outs_ref[1]
        hop_out[2] = outs_ref[0]


def store_by_owner(core, slot, refs, index, value):
    left_same, left_other, right_same, right_other, own_other, own_same = refs
    same, other = ((left_same, left_other), (own_same, own_other), (right_same, right_other))[slot // 2]

    @pl.when(core == slot % 2)
    def _():
        same[index] = value

    @pl.when(core != slot % 2)
    def _():
        other[index] = value


def last_kernel(hop_ref, skip0_ref, skip1_ref, ct_ref, outs_in, inflow_in, *refs):
    refs, refs_out = refs[:6], refs[6:]
    owners, (hop_out, sent_out, up_ref) = refs_out[:6], refs_out[6:9]
    packed, outs_ref, inflow_ref, state_ref, pre_ref, sent_ref, grad_ref, sems = refs_out[9:]
    here, core = position()

    @pl.when(here == LAST)
    def _():
        weights = Weights(core, refs, packed, sems)
        for pair in range(3):
            weights.start(pair)
        skips = [hop_ref.at[1], hop_ref.at[2], skip1_ref.at[1], skip1_ref.at[0], skip0_ref.at[1], skip0_ref.at[0]]
        for slot in range(6):
            weights.wait(slot)
            state = (hop_ref[0] if slot == 0 else outs_ref[slot - 1]).astype(F32)
            state = state + skips[slot][...].astype(F32)
            inflow_ref[slot] = state.astype(BF16)
            weights.forward(slot, state, state_ref, pre_ref, outs_ref)
        for slot in reversed(range(6)):
            up_ref[slot] = ct_ref[...] if slot == 5 else sent_ref[slot + 1]
            grad = up_ref[slot].astype(F32)
            sent_ref[slot] = weights.backward(slot, grad, state_ref, pre_ref, grad_ref)
        hop_out[...] = sent_ref[:2]
        sent_out[...] = sent_ref[2:]
        for slot in range(6):
            store_by_owner(core, slot, owners, 0, outs_ref[slot])
            store_by_owner(core, slot, owners, 1, inflow_ref[slot])

    @pl.when((here == SECOND) | (here == MIDDLE))
    def _():
        for slot in range(6):
            store_by_owner(core, slot, owners, 0, outs_in[slot])
            store_by_owner(core, slot, owners, 1, inflow_in[slot])


def middle_backward_kernel(hop_ref, state_ref, pre_ref, *refs):
    refs, (hop_out, up_ref, packed, sent_ref, grad_ref, sems) = refs[:6], refs[6:]
    here, core = position()

    @pl.when(here == MIDDLE)
    def _():
        weights = Weights(core, refs, packed, sems)
        for pair in reversed(range(3)):
            weights.start(pair)
        skips = [hop_ref.at[1], hop_ref.at[0], sent_ref.at[5], sent_ref.at[4]]
        for slot in reversed(range(6)):
            weights.wait(slot)
            grad = (hop_ref[0] if slot == 5 else sent_ref[slot + 1]).astype(F32)
            if slot < 4:
                grad = grad + skips[slot][...].astype(F32)
            up_ref[slot] = grad.astype(BF16)
            sent_ref[slot] = weights.backward(slot, grad, state_ref, pre_ref, grad_ref)
        hop_out[...] = sent_ref[0]


def first_backward_kernel(hop_ref, skip_ref, state_ref, pre_ref, up_middle, up_last, *refs):
    refs, refs_out = refs[:4], refs[4:]
    owners, (packed, sent_ref, grad_ref, sems) = refs_out[:6], refs_out[6:]
    here, core = position()
    everything = (slice(None), slice(None))

    @pl.when(here == SECOND)
    def _():
        weights = Weights(core, refs, packed, sems)
        for pair in reversed(range(2)):
            weights.start(pair)
        for slot in reversed(range(4)):
            weights.wait(slot)
            grad = (hop_ref[...] if slot == 3 else sent_ref[slot + 1]).astype(F32)
            grad = grad + skip_ref[3 - slot].astype(F32)
            store_by_owner(core, slot, owners, everything, grad.astype(BF16))
            if slot:
                sent_ref[slot] = weights.backward(slot, grad, state_ref, pre_ref, grad_ref)

    for chip, source in ((MIDDLE, up_middle), (LAST, up_last)):

        @pl.when(here == chip)
        def _():
            for slot in range(6):
                store_by_owner(core, slot, owners, everything, source[slot])


def owner_kernel(counts, g_ref, w_in_ref, w_out_ref, *refs):
    rows, ups, (out_ref, parts_ref, inflow_ref, grad_ref, gw_ref) = refs[:6], refs[6:12], refs[12:]
    here, core = position()
    active = (here == SECOND) | (here == MIDDLE) | (here == LAST)

    def arrived(refs, index):
        left_same, left_other, right_same, right_other, own_other, own_same = [ref[index].astype(F32) for ref in refs]
        same = left_same + right_same + jnp.where(active, own_same, 0.0)
        return same, left_other + right_other + own_other

    pixels = grad_ref.shape[0] // 2
    at_same = pl.ds(pl.multiple_of(core * pixels, pixels), pixels)
    at_other = pl.ds(pl.multiple_of((1 - core) * pixels, pixels), pixels)
    same, other = arrived(rows, 0)
    out_ref[core] = same.astype(BF16)
    out_ref[1 - core] = other.astype(BF16)
    same, other = arrived(rows, 1)
    inflow_ref[at_same] = same
    inflow_ref[at_other] = other
    same, other = arrived(ups, (slice(None), slice(None)))
    grad_ref[at_same] = same
    grad_ref[at_other] = other

    inflow = inflow_ref[...]
    after, pre0 = layer_forward(inflow, g_ref[0][None], w_in_ref[0], w_out_ref[0])

    def gradients(layer, state, pre, grad):
        gain = g_ref[layer][None]
        grad_cast = grad.astype(BF16)
        d_act = dot_t(grad_cast, w_out_ref[layer])
        sig = jax.nn.sigmoid(pre)
        act = (pre * sig).astype(BF16)
        d_pre = (d_act * (sig * (1.0 + pre * (1.0 - sig)))).astype(BF16)
        scale = scale_of(state)
        unit = state * scale
        normed = (unit * gain).astype(BF16)
        gw_ref[layer] = dot_rows(normed, d_pre)
        gw_ref[2 + layer] = dot_rows(act, grad_cast)
        return scale, unit, d_pre, gain

    @pl.when(counts[0] > 1)
    def _():
        grad = grad_ref[...]
        pre1 = dot((after * scale_of(after) * g_ref[1][None]).astype(BF16), w_in_ref[1])
        scale, unit, d_pre, gain = gradients(1, after, pre1, grad)
        d_unit = dot_t(d_pre, w_in_ref[1]) * gain
        inner = jnp.mean(d_unit * unit, axis=-1, keepdims=True)
        grad_ref[...] = grad + scale * (d_unit - unit * inner)

    @pl.when(counts[0] <= 1)
    def _():
        gw_ref[1] = jnp.zeros((C, C), F32)
        gw_ref[3] = jnp.zeros((C, C), F32)

    gradients(0, inflow, pre0, grad_ref[...])

    columns, double, _ = parts_ref.shape
    for matrix in range(2):
        both = [gw_ref[2 * matrix + layer].reshape(columns, double // 2, C) for layer in range(2)]
        parts_ref[:, :, matrix * C : (matrix + 1) * C] = jnp.concatenate(both, 1).astype(BF16)


def sum_kernel(parts_ref, w_ref, g_ref, gw_in_ref, gw_out_ref, gain_ref):
    columns, double, _ = parts_ref.shape
    total = parts_ref[0].astype(F32)
    for source in range(1, columns):
        total = total + parts_ref[source].astype(F32)
    share = double // 2
    for layer in range(2):
        rows = total[layer * share : (layer + 1) * share]
        gw_in_ref[layer] = rows[:, :C]
        gw_out_ref[layer] = rows[:, C:]
        product = jnp.sum(rows[:, :C] * w_ref[layer], axis=1, keepdims=True)
        gain_ref[layer] = product / g_ref[layer]


def vmem():
    return pl.BlockSpec(memory_space=pltpu.VMEM)


def smem():
    return pl.BlockSpec(memory_space=pltpu.SMEM)


def hbm():
    return pl.BlockSpec(memory_space=pl.ANY)


def call(kernel, name, inputs, outputs, scratch=(), flops=10**8):
    specs = {"vmem": vmem, "smem": smem, "hbm": hbm}
    outputs = [jax.ShapeDtypeStruct(shape, dtype) for shape, dtype in outputs]
    return pl.pallas_call(
        kernel,
        out_shape=outputs,
        in_specs=[specs[memory]() for memory, _ in inputs],
        out_specs=[vmem() for _ in outputs],
        scratch_shapes=list(scratch),
        compiler_params=pltpu.CompilerParams(vmem_limit_bytes=32 * 2**20),
        cost_estimate=pl.CostEstimate(flops=flops, bytes_accessed=2**20, transcendentals=0),
        name=name,
    )(*[array for _, array in inputs])


def at_vmem(*arrays):
    return [("vmem", array) for array in arrays]


def at_hbm(*arrays):
    return [("hbm", array) for array in arrays]


def move(value, chips, cross=False):
    pairs = [(2 * a + core, 2 * b + (1 - core if cross else core)) for a, b in chips for core in range(2)]
    return lax.ppermute(value, "section", pairs)


def packed_scratch(slots):
    return pltpu.VMEM((slots, PACK, C), BF16)


def kept(slots, pixels):
    return pltpu.VMEM((slots, 2, pixels, C), F32)


def body(images, cotangent, w_in, w_out, gains, layer_counts):
    columns = lax.axis_size("dp")
    core = lax.axis_index("section") % 2
    micro, pixels, _ = images.shape
    tile = (pixels, C)
    dma = pltpu.SemaphoreType.DMA
    x = lax.dynamic_index_in_dim(images, core, 0, keepdims=False)
    ct = lax.dynamic_index_in_dim(cotangent, core, 0, keepdims=False)

    (own,) = call(pack_kernel, "pack", [("smem", layer_counts)] + at_vmem(w_in[0], w_out[0], gains[0]), [((PACK, C), BF16)])
    partner = move(own, [(chip, chip) for chip in (FIRST, SECOND, MIDDLE, LAST)], cross=True)
    left = move(own, [(chip - 1, chip) for chip in (SECOND, MIDDLE, LAST)])
    right = move(own, [(chip + 1, chip) for chip in (MIDDLE, LAST)])

    def pair(chip, value):
        return call(
            lambda *refs: pair_kernel(chip, *refs),
            "pair_forward",
            at_vmem(value) + at_hbm(own, partner),
            [((2,) + tile, BF16), (tile, BF16)],
            [packed_scratch(2), kept(2, pixels), kept(2, pixels), dma((2,))],
        )

    outs_a, last_a = pair(FIRST, x)
    outs_b, last_b = pair(SECOND, move(last_a, [(FIRST, SECOND)]))
    hop = move(last_b, [(SECOND, MIDDLE)])
    skip0 = move(outs_a, [(FIRST, LAST)])
    skip1 = move(outs_b, [(SECOND, LAST)])
    left_partner = move(left, [(chip, chip) for chip in (SECOND, MIDDLE, LAST)], cross=True)
    right_partner = move(right, [(chip, chip) for chip in (MIDDLE, LAST)], cross=True)
    weights = at_hbm(left, left_partner, own, partner, right, right_partner)
    six, state_shape = (6,) + tile, (6, 2) + tile

    outs, inflows, hop, states, pres = call(
        middle_forward_kernel,
        "middle_forward",
        at_vmem(x, hop) + weights,
        [(six, BF16), (six, BF16), ((3,) + tile, BF16), (state_shape, F32), (state_shape, F32)],
        [packed_scratch(6), dma((6,))],
    )
    hop = move(hop, [(MIDDLE, LAST)])
    *to_owners, hop, skips, ups_last = call(
        last_kernel,
        "last_both",
        at_vmem(hop, skip0, skip1, ct, outs, inflows) + weights,
        [((2,) + tile, BF16)] * 6 + [((2,) + tile, BF16), ((4,) + tile, BF16), (six, BF16)],
        [
            packed_scratch(6),
            pltpu.VMEM(six, BF16),
            pltpu.VMEM(six, BF16),
            kept(6, pixels),
            kept(6, pixels),
            pltpu.VMEM(six, BF16),
            pltpu.VMEM(tile, F32),
            dma((6,)),
        ],
    )
    hop = move(hop, [(LAST, MIDDLE)])
    skips = move(skips, [(LAST, SECOND)])

    def deliver(values):
        left_same, left_other, right_same, right_other, own_other, own_same = values
        lefts = [(chip, chip - 1) for chip in (SECOND, MIDDLE, LAST)]
        rights = [(chip, chip + 1) for chip in (MIDDLE, LAST)]
        owns = [(chip, chip) for chip in (SECOND, MIDDLE, LAST)]
        return [
            move(left_same, lefts),
            move(left_other, lefts, cross=True),
            move(right_same, rights),
            move(right_other, rights, cross=True),
            move(own_other, owns, cross=True),
            own_same,
        ]

    rows = deliver(to_owners)
    hop, ups_middle = call(
        middle_backward_kernel,
        "middle_backward",
        at_vmem(hop, states, pres) + weights,
        [(tile, BF16), (six, BF16)],
        [packed_scratch(6), pltpu.VMEM(six, BF16), pltpu.VMEM(tile, F32), dma((6,))],
    )
    hop = move(hop, [(MIDDLE, SECOND)])
    to_owners = call(
        first_backward_kernel,
        "first_backward",
        at_vmem(hop, skips, states, pres, ups_middle, ups_last) + weights[:4],
        [(tile, BF16)] * 6,
        [packed_scratch(4), pltpu.VMEM((4,) + tile, BF16), pltpu.VMEM(tile, F32), dma((4,))],
    )
    ups = deliver(to_owners)

    share = C // columns
    section_outputs, parts = call(
        owner_kernel,
        "owner_gradients",
        [("smem", layer_counts)] + at_vmem(gains[0], w_in[0], w_out[0], *rows, *ups),
        [((micro, pixels, C), BF16), ((columns, 2 * share, 2 * C), BF16)],
        [pltpu.VMEM((micro * pixels, C), F32)] * 2 + [pltpu.VMEM((4, C, C), F32)],
    )
    parts = lax.all_to_all(parts, "dp", 0, 0, tiled=True)
    start = lax.axis_index("dp") * share
    w_rows = lax.dynamic_slice_in_dim(w_in[0], start, share, 1).astype(F32)
    gain_rows = lax.dynamic_slice_in_dim(gains[0], start, share, 1)[:, :, None]
    grad_in, grad_out, grad_gain = call(
        sum_kernel,
        "sum_parts",
        at_vmem(parts, w_rows, gain_rows),
        [((2, share, C), F32), ((2, share, C), F32), ((2, share, 1), F32)],
    )
    return section_outputs[None], grad_in[None], grad_out[None], grad_gain[None, :, :, 0]


def solution(mesh):
    return jax.shard_map(
        body,
        mesh=mesh,
        in_specs=(
            P(None, "dp", None),
            P(None, "dp", None),
            P("section", None, None, None),
            P("section", None, None, None),
            P("section", None, None),
            P("section"),
        ),
        out_specs=(
            P("section", None, "dp", None),
            P("section", None, "dp", None),
            P("section", None, "dp", None),
            P("section", None, "dp"),
        ),
        check_vma=False,
    )
```

```python
import jax
import jax.numpy as jnp
from jax import lax
from jax.experimental import pallas as pl
from jax.experimental.pallas import tpu as pltpu
from jax.sharding import PartitionSpec as P

C = 256
EPS = 1e-06
F32 = jnp.float32
BF16 = jnp.bfloat16
PACK = 4 * C + 16
FIRST, SECOND, MIDDLE, LAST = 0, 1, 3, 6


def dot(a, b):
    return jnp.dot(a, b, preferred_element_type=F32)


def dot_t(a, b):
    return lax.dot_general(a, b, (((1,), (1,)), ((), ())), preferred_element_type=F32)


def dot_rows(a, b):
    return lax.dot_general(a, b, (((0,), (0,)), ((), ())), preferred_element_type=F32)


def scale_of(state):
    return lax.rsqrt(jnp.mean(state * state, axis=-1, keepdims=True) + EPS)


def layer_forward(state, gain, first, second):
    normed = (state * scale_of(state) * gain).astype(BF16)
    pre = dot(normed, first)
    act = (pre * jax.nn.sigmoid(pre)).astype(BF16)
    return state + dot(act, second), pre


def layer_backward(grad, state, pre, gain, first, second):
    d_act = dot_t(grad.astype(BF16), second)
    sig = jax.nn.sigmoid(pre)
    slope = sig * (1.0 + pre * (1.0 - sig))
    d_pre = (d_act * slope).astype(BF16)
    d_normed = dot_t(d_pre, first)
    scale = scale_of(state)
    unit = state * scale
    d_unit = d_normed * gain
    inner = jnp.mean(d_unit * unit, axis=-1, keepdims=True)
    return grad + scale * (d_unit - unit * inner)


def position():
    here = lax.axis_index("section")
    return here // 2, here % 2


class Weights:
    def __init__(self, core, refs, packed, sems):
        self.refs, self.packed, self.sems, self.core = refs, packed, sems, core

    def copy(self, ref, slot):
        return pltpu.make_async_copy(ref, self.packed.at[slot], self.sems.at[slot])

    def start(self, pair):
        same, other = self.refs[2 * pair], self.refs[2 * pair + 1]
        self.copy(same, 2 * pair + self.core).start()
        self.copy(other, 2 * pair + 1 - self.core).start()

    def wait(self, slot):
        self.copy(self.refs[0], slot).wait()

    def tail(self, slot):
        return self.packed[slot, 4 * C :].astype(F32)

    def gain(self, slot, layer):
        tail = self.tail(slot)
        return tail[layer : layer + 1] + tail[2 + layer : 3 + layer] + tail[4 + layer : 5 + layer]

    def first(self, slot, layer):
        return self.packed[slot, layer * C : (layer + 1) * C]

    def second(self, slot, layer):
        return self.packed[slot, (2 + layer) * C : (3 + layer) * C]

    def both(self, slot):
        return jnp.max(self.tail(slot)[8:9]) > 1.5

    def forward(self, slot, state, state_ref, pre_ref, out_ref):
        state_ref[slot, 0] = state
        state, pre = layer_forward(state, self.gain(slot, 0), self.first(slot, 0), self.second(slot, 0))
        pre_ref[slot, 0] = pre
        out_ref[slot] = state.astype(BF16)

        @pl.when(self.both(slot))
        def _():
            state_ref[slot, 1] = state
            after, pre = layer_forward(state, self.gain(slot, 1), self.first(slot, 1), self.second(slot, 1))
            pre_ref[slot, 1] = pre
            out_ref[slot] = after.astype(BF16)

    def backward(self, slot, grad, state_ref, pre_ref, grad_ref):
        grad_ref[...] = grad

        def layer(number):
            return layer_backward(
                grad_ref[...],
                state_ref[slot, number],
                pre_ref[slot, number],
                self.gain(slot, number),
                self.first(slot, number),
                self.second(slot, number),
            )

        @pl.when(self.both(slot))
        def _():
            grad_ref[...] = layer(1)

        return layer(0).astype(BF16)


def pack_kernel(counts, w_in_ref, w_out_ref, g_ref, packed_ref, tail_ref, sems):
    copies = [
        pltpu.make_async_copy(ref.at[layer], packed_ref.at[pl.ds((2 * side + layer) * C, C)], sems.at[2 * side + layer])
        for side, ref in enumerate((w_in_ref, w_out_ref))
        for layer in range(2)
    ]
    for copy in copies:
        copy.start()
    gains = g_ref[...]
    coarse = gains.astype(BF16).astype(F32)
    rest = gains - coarse
    fine = rest.astype(BF16).astype(F32)
    count = jnp.full((2, C), counts[0].astype(F32))
    rows = [coarse, fine, rest - fine, jnp.zeros_like(coarse), count, jnp.zeros((6, C), F32)]
    tail_ref[...] = jnp.concatenate(rows, 0).astype(BF16)
    copies.append(pltpu.make_async_copy(tail_ref, packed_ref.at[pl.ds(4 * C, 16)], sems.at[4]))
    copies[-1].start()
    for copy in copies:
        copy.wait()


def pair_kernel(chip, x_ref, same, other, outs_ref, last_ref, rows_same, rows_other, packed, states, pres, sems):
    here, core = position()

    def keep(slot, index, value):
        @pl.when(core == slot)
        def _():
            rows_same[index] = value

        @pl.when(core != slot)
        def _():
            rows_other[index] = value

    @pl.when(here == chip)
    def _():
        weights = Weights(core, [same, other], packed, sems)
        weights.start(0)
        state = (x_ref[core] if chip == FIRST else x_ref[...]).astype(F32)
        for slot in range(2):
            weights.wait(slot)
            weights.forward(slot, state, states, pres, outs_ref)
            keep(slot, 0, outs_ref[slot])
            keep(slot, 1, state.astype(BF16))
            state = outs_ref[slot].astype(F32)
        last_ref[...] = outs_ref[1]


def middle_forward_kernel(hop_ref, *refs):
    refs, (outs_ref, inflow_ref, hop_out, state_ref, pre_ref, packed, sems) = refs[:6], refs[6:]
    here, core = position()

    @pl.when(here == MIDDLE)
    def _():
        weights = Weights(core, refs, packed, sems)
        for pair in range(3):
            weights.start(pair)
        for slot in range(6):
            weights.wait(slot)
            state = (hop_ref[...] if slot == 0 else outs_ref[slot - 1]).astype(F32)
            if slot >= 4:
                state = state + outs_ref[7 - slot].astype(F32)
            inflow_ref[slot] = state.astype(BF16)
            weights.forward(slot, state, state_ref, pre_ref, outs_ref)
        hop_out[0] = outs_ref[5]
        hop_out[1:] = outs_ref[:2]


def store_by_owner(core, slot, refs, index, value):
    left_same, left_other, right_same, right_other, own_other, own_same = refs
    same, other = ((left_same, left_other), (own_same, own_other), (right_same, right_other))[slot // 2]

    @pl.when(core == slot % 2)
    def _():
        same[index] = value

    @pl.when(core != slot % 2)
    def _():
        other[index] = value


def last_kernel(hop_ref, skip0_ref, skip1_ref, ct_ref, outs_in, inflow_in, *refs):
    refs, refs_out = refs[:6], refs[6:]
    owners, (hop_out, sent_out, up_ref) = refs_out[:6], refs_out[6:9]
    packed, outs_ref, inflow_ref, state_ref, pre_ref, sent_ref, grad_ref, sems = refs_out[9:]
    here, core = position()

    def keep_rows(slots, outs, inflows):
        for slot in slots:
            store_by_owner(core, slot, owners, 0, outs[slot])
            store_by_owner(core, slot, owners, 1, inflows[slot])

    @pl.when(here == LAST)
    def _():
        weights = Weights(core, refs, packed, sems)
        for pair in range(3):
            weights.start(pair)
        skips = [hop_ref.at[2], hop_ref.at[1]] + [ref.at[index] for ref in (skip1_ref, skip0_ref) for index in (1, 0)]
        for slot in range(6):
            weights.wait(slot)
            state = (hop_ref[0] if slot == 0 else outs_ref[slot - 1]).astype(F32)
            state = state + skips[slot][...].astype(F32)
            inflow_ref[slot] = state.astype(BF16)
            weights.forward(slot, state, state_ref, pre_ref, outs_ref)
        for slot in reversed(range(6)):
            up_ref[slot] = ct_ref[core] if slot == 5 else sent_ref[slot + 1]
            grad = up_ref[slot].astype(F32)
            sent_ref[slot] = weights.backward(slot, grad, state_ref, pre_ref, grad_ref)
        hop_out[...] = sent_ref[:2]
        sent_out[...] = sent_ref[2:]
        keep_rows(range(6), outs_ref, inflow_ref)

    @pl.when(here == MIDDLE)
    def _():
        keep_rows(range(6), outs_in, inflow_in)


def middle_backward_kernel(hop_ref, state_ref, pre_ref, x_ref, *refs):
    refs, low_refs, refs_out = refs[:6], refs[6:8] + refs[2:4], refs[8:]
    hop_out, up_ref, low_state, low_pre, packed, sent_ref, grad_ref, sems = refs_out
    here, core = position()

    @pl.when(here == SECOND)
    def _():
        weights = Weights(core, low_refs, packed, sems)
        for pair in range(2):
            weights.start(pair)
        for slot in range(4):
            weights.wait(slot)
            state = (x_ref[core] if slot == 0 else sent_ref[slot - 1]).astype(F32)
            weights.forward(slot, state, low_state, low_pre, sent_ref)

    @pl.when(here == MIDDLE)
    def _():
        weights = Weights(core, refs, packed, sems)
        for pair in reversed(range(3)):
            weights.start(pair)
        skips = [hop_ref.at[1], hop_ref.at[0], sent_ref.at[5], sent_ref.at[4]]
        for slot in reversed(range(6)):
            weights.wait(slot)
            grad = (hop_ref[0] if slot == 5 else sent_ref[slot + 1]).astype(F32)
            if slot < 4:
                grad = grad + skips[slot][...].astype(F32)
            up_ref[slot] = grad.astype(BF16)
            sent_ref[slot] = weights.backward(slot, grad, state_ref, pre_ref, grad_ref)
        hop_out[...] = sent_ref[0]


def first_backward_kernel(hop_ref, skip_ref, state_ref, pre_ref, up_middle, up_last, *refs):
    rows, refs, refs_out = refs[:6], refs[6:10], refs[10:]
    away, own, (packed, sent_ref, grad_ref, sems, role_sems) = refs_out[:4], refs_out[4:6], refs_out[6:]
    here, core = position()
    owners = list(away) + [ref.at[2] for ref in own]

    def rows_copies(other, same):
        return [
            pltpu.make_async_copy(source, target.at[pl.ds(0, 2)], role_sems.at[number])
            for number, (source, target) in enumerate(zip((other, same), own))
        ]

    for chips, (other, same) in (
        ((here == MIDDLE) | (here == LAST), rows[:2]),
        (here == FIRST, (rows[3], rows[2])),
        (here == SECOND, (rows[5], rows[4])),
    ):

        @pl.when(chips)
        def _():
            for copy in rows_copies(other, same):
                copy.start()

    everything = (slice(None), slice(None))

    @pl.when(here == SECOND)
    def _():
        weights = Weights(core, refs, packed, sems)
        for pair in reversed(range(2)):
            weights.start(pair)
        for slot in reversed(range(4)):
            weights.wait(slot)
            grad = (hop_ref[...] if slot == 3 else sent_ref[slot + 1]).astype(F32)
            grad = grad + skip_ref[3 - slot].astype(F32)
            store_by_owner(core, slot, owners, everything, grad.astype(BF16))
            if slot:
                sent_ref[slot] = weights.backward(slot, grad, state_ref, pre_ref, grad_ref)

    for chip, source in ((MIDDLE, up_middle), (LAST, up_last)):

        @pl.when(here == chip)
        def _():
            for slot in range(6):
                store_by_owner(core, slot, owners, everything, source[slot])

    @pl.when((here <= SECOND) | (here == MIDDLE) | (here == LAST))
    def _():
        for copy in rows_copies(*rows[:2]):
            copy.wait()


def owner_kernel(counts, g_ref, w_in_ref, w_out_ref, *refs):
    pieces, (out_ref, parts_ref, inflow_ref, grad_ref, gw_ref) = refs[:10], refs[10:]
    rows, ups, own = pieces[:4], pieces[4:8], (pieces[9], pieces[8])
    here, core = position()
    pixels = grad_ref.shape[0] // 2
    places = [pl.ds(pl.multiple_of(side * pixels, pixels), pixels) for side in (core, 1 - core)]
    everything = (slice(None), slice(None))

    def take_rows(chips, refs):
        @pl.when(chips)
        def _():
            for ref, side, place in zip(refs, (core, 1 - core), places):
                out_ref[side] = ref[0]
                inflow_ref[place] = ref[1].astype(F32)

    def take_ups(chips, refs, index):
        @pl.when(chips)
        def _():
            for ref, place in zip(refs, places):
                grad_ref[place] = ref[index].astype(F32)

    holds = (here == SECOND) | (here == MIDDLE) | (here == LAST)
    take_rows(holds | (here == FIRST), own)
    take_rows((here == MIDDLE - 1) | (here == LAST - 1), rows[:2])
    take_rows((here == MIDDLE + 1) | (here == LAST + 1), rows[2:])
    take_ups(holds, own, 2)
    take_ups((here == SECOND - 1) | (here == MIDDLE - 1) | (here == LAST - 1), ups[:2], everything)
    take_ups((here == MIDDLE + 1) | (here == LAST + 1), ups[2:], everything)

    inflow = inflow_ref[...]
    after, pre0 = layer_forward(inflow, g_ref[0][None], w_in_ref[0], w_out_ref[0])

    def gradients(layer, state, pre, grad):
        gain = g_ref[layer][None]
        grad_cast = grad.astype(BF16)
        d_act = dot_t(grad_cast, w_out_ref[layer])
        sig = jax.nn.sigmoid(pre)
        act = (pre * sig).astype(BF16)
        d_pre = (d_act * (sig * (1.0 + pre * (1.0 - sig)))).astype(BF16)
        scale = scale_of(state)
        unit = state * scale
        normed = (unit * gain).astype(BF16)
        gw_ref[layer] = dot_rows(normed, d_pre)
        gw_ref[2 + layer] = dot_rows(act, grad_cast)
        return scale, unit, d_pre, gain

    @pl.when(counts[0] > 1)
    def _():
        grad = grad_ref[...]
        pre1 = dot((after * scale_of(after) * g_ref[1][None]).astype(BF16), w_in_ref[1])
        scale, unit, d_pre, gain = gradients(1, after, pre1, grad)
        d_unit = dot_t(d_pre, w_in_ref[1]) * gain
        inner = jnp.mean(d_unit * unit, axis=-1, keepdims=True)
        grad_ref[...] = grad + scale * (d_unit - unit * inner)

    @pl.when(counts[0] <= 1)
    def _():
        gw_ref[1] = jnp.zeros((C, C), F32)
        gw_ref[3] = jnp.zeros((C, C), F32)

    gradients(0, inflow, pre0, grad_ref[...])

    columns, double, _ = parts_ref.shape
    for matrix in range(2):
        both = [gw_ref[2 * matrix + layer].reshape(columns, double // 2, C) for layer in range(2)]
        parts_ref[:, :, matrix * C : (matrix + 1) * C] = jnp.concatenate(both, 1).astype(BF16)


def sum_kernel(parts_ref, w_ref, g_ref, gw_in_ref, gw_out_ref, gain_ref):
    columns, double, _ = parts_ref.shape
    total = parts_ref[0].astype(F32)
    for source in range(1, columns):
        total = total + parts_ref[source].astype(F32)
    share = double // 2
    for layer in range(2):
        rows = total[layer * share : (layer + 1) * share]
        gw_in_ref[layer] = rows[:, :C]
        gw_out_ref[layer] = rows[:, C:]
        product = rows[:, :C] * w_ref[layer]
        ones = jnp.ones((1, C), F32)
        product = lax.dot_general(
            ones, product, (((1,), (1,)), ((), ())), precision=lax.Precision.HIGHEST, preferred_element_type=F32
        )
        gain_ref[layer : layer + 1] = product / g_ref[layer : layer + 1]


def vmem():
    return pl.BlockSpec(memory_space=pltpu.VMEM)


def smem():
    return pl.BlockSpec(memory_space=pltpu.SMEM)


def hbm():
    return pl.BlockSpec(memory_space=pltpu.HBM)


def call(kernel, name, inputs, outputs, scratch=(), us=1, limit=32 * 2**20):
    specs = {"vmem": vmem, "smem": smem, "hbm": hbm}
    outputs = [jax.ShapeDtypeStruct(shape, dtype) for shape, dtype in outputs]
    return pl.pallas_call(
        kernel,
        out_shape=outputs,
        in_specs=[specs[memory]() for memory, _ in inputs],
        out_specs=[vmem() for _ in outputs],
        scratch_shapes=list(scratch),
        compiler_params=pltpu.CompilerParams(vmem_limit_bytes=limit),
        cost_estimate=pl.CostEstimate(flops=us * 10**9, bytes_accessed=2**20, transcendentals=0),
        name=name,
    )(*[array for _, array in inputs])


def at_vmem(*arrays):
    return [("vmem", array) for array in arrays]


def at_hbm(*arrays):
    return [("hbm", array) for array in arrays]


def move(value, chips, cross=False):
    pairs = [(2 * a + core, 2 * b + (1 - core if cross else core)) for a, b in chips for core in range(2)]
    return lax.ppermute(value, "section", pairs)


def packed_scratch(slots):
    return pltpu.VMEM((slots, PACK, C), BF16)


def kept(slots, pixels):
    return pltpu.VMEM((slots, 2, pixels, C), F32)


def body(images, cotangent, w_in, w_out, gains, layer_counts):
    columns = lax.axis_size("dp")
    micro, pixels, _ = images.shape
    tile = (pixels, C)
    dma = pltpu.SemaphoreType.DMA
    barrier = lax.optimization_barrier

    (own,) = call(
        pack_kernel,
        "pack",
        [("smem", layer_counts)] + at_hbm(w_in[0], w_out[0]) + at_vmem(gains[0]),
        [((PACK, C), BF16)],
        [pltpu.VMEM((16, C), BF16), dma((5,))],
    )
    holders = (MIDDLE, LAST)
    partner = move(own, [(chip, chip) for chip in (FIRST, SECOND, MIDDLE, LAST)], cross=True)
    left = move(own, [(chip - 1, chip) for chip in holders])
    right = move(own, [(chip + 1, chip) for chip in holders])

    def pair(chip, value):
        return call(
            lambda *refs: pair_kernel(chip, *refs),
            "pair_forward",
            at_vmem(value) + at_hbm(own, partner),
            [((2,) + tile, BF16), (tile, BF16)] + [((2,) + tile, BF16)] * 2,
            [packed_scratch(2), kept(2, pixels), kept(2, pixels), dma((2,))],
        )

    outs_a, last_a, *rows_a = pair(FIRST, images)
    outs_b, last_b, *rows_b = pair(SECOND, move(last_a, [(FIRST, SECOND)]))
    hop = move(last_b, [(SECOND, MIDDLE)])
    left, right, later, hop = barrier((left, right, own, hop))
    left_partner = move(left, [(chip, chip) for chip in holders], cross=True)
    right_partner = move(right, [(chip, chip) for chip in holders], cross=True)
    weights = at_hbm(left, left_partner, own, partner, right, right_partner)
    four, six = (4,) + tile, (6,) + tile
    four_state, six_state = (4, 2) + tile, (6, 2) + tile

    outs, inflows, hop, states, pres = call(
        middle_forward_kernel,
        "middle_forward",
        at_vmem(hop) + weights,
        [(six, BF16), (six, BF16), ((3,) + tile, BF16), (six_state, F32), (six_state, F32)],
        [packed_scratch(6), dma((6,))],
        us=3,
    )
    skip0, skip1, hop = barrier((outs_a, outs_b, hop))
    hop = move(hop, [(MIDDLE, LAST)])
    skip0 = move(skip0, [(FIRST, LAST)])
    skip1 = move(skip1, [(SECOND, LAST)])
    low_left = move(later, [(SECOND - 1, SECOND)])
    low_partner = move(low_left, [(SECOND, SECOND)], cross=True)
    low_weights = at_hbm(low_left, low_partner, own, partner)
    *to_owners, hop, skips, ups_last = call(
        last_kernel,
        "last_both",
        at_vmem(hop, skip0, skip1, cotangent, outs, inflows) + weights,
        [((2,) + tile, BF16)] * 6 + [((2,) + tile, BF16), (four, BF16), (six, BF16)],
        [
            packed_scratch(6),
            pltpu.VMEM(six, BF16),
            pltpu.VMEM(six, BF16),
            kept(6, pixels),
            kept(6, pixels),
            pltpu.VMEM(six, BF16),
            pltpu.VMEM(tile, F32),
            dma((6,)),
        ],
        us=8,
    )
    hop = move(hop, [(LAST, MIDDLE)])
    skips = move(skips, [(LAST, SECOND)])

    def deliver(chips, *pieces):
        lefts = [(chip, chip - 1) for chip in chips]
        rights = [(chip, chip + 1) for chip in (MIDDLE, LAST)]
        routes = ((lefts, False), (lefts, True), (rights, False), (rights, True))
        return [move(piece, *route) for piece, route in zip(pieces, routes) if piece is not None]

    *away, rows_other, rows_same = to_owners
    rows_left, rows_right = away[:2], deliver((MIDDLE, LAST), None, None, *away[2:])
    hop, rows_right = barrier((hop, rows_right))
    hop, ups_middle, low_states, low_pres = call(
        middle_backward_kernel,
        "middle_backward",
        at_vmem(hop, states, pres, images) + weights + low_weights[:2],
        [(tile, BF16), (six, BF16), (four_state, F32), (four_state, F32)],
        [packed_scratch(6), pltpu.VMEM(six, BF16), pltpu.VMEM(tile, F32), dma((6,))],
        us=5,
    )
    rows_left, hop = barrier((rows_left, hop))
    hop = move(hop, [(MIDDLE, SECOND)])
    rows_left = deliver((MIDDLE, LAST), *rows_left, None, None)
    rows = rows_left + rows_right
    *away, own_other, own_same = call(
        first_backward_kernel,
        "first_backward",
        at_vmem(hop, skips, low_states, low_pres, ups_middle, ups_last)
        + at_hbm(rows_other, rows_same, *rows_a, *rows_b)
        + low_weights,
        [(tile, BF16)] * 4 + [((3,) + tile, BF16)] * 2,
        [packed_scratch(4), pltpu.VMEM(four, BF16), pltpu.VMEM(tile, F32), dma((4,)), dma((2,))],
        us=3,
    )
    ups = deliver((SECOND, MIDDLE, LAST), *away)
    own_other = move(own_other, [(chip, chip) for chip in (FIRST, SECOND, MIDDLE, LAST)], cross=True)

    share = C // columns
    section_outputs, parts = call(
        owner_kernel,
        "owner_gradients",
        [("smem", layer_counts)] + at_vmem(gains[0], w_in[0], w_out[0], *rows, *ups, own_other, own_same),
        [((micro, pixels, C), BF16), ((columns, 2 * share, 2 * C), BF16)],
        [pltpu.VMEM((micro * pixels, C), F32)] * 2 + [pltpu.VMEM((4, C, C), F32)],
    )
    parts = lax.all_to_all(parts, "dp", 0, 0, tiled=True)
    start = lax.axis_index("dp") * share
    w_rows = lax.dynamic_slice_in_dim(w_in[0], start, share, 1).astype(F32)
    gain_rows = lax.dynamic_slice_in_dim(gains[0], start, share, 1)
    grad_in, grad_out, grad_gain = call(
        sum_kernel,
        "sum_parts",
        at_vmem(parts, w_rows, gain_rows),
        [((2, share, C), F32), ((2, share, C), F32), ((2, share), F32)],
    )
    return section_outputs[None], grad_in[None], grad_out[None], grad_gain[None]


def solution(mesh):
    return jax.shard_map(
        body,
        mesh=mesh,
        in_specs=(
            P(None, "dp", None),
            P(None, "dp", None),
            P("section", None, None, None),
            P("section", None, None, None),
            P("section", None, None),
            P("section"),
        ),
        out_specs=(
            P("section", None, "dp", None),
            P("section", None, "dp", None),
            P("section", None, "dp", None),
            P("section", None, "dp"),
        ),
        check_vma=False,
    )
```

```python
import functools

import jax
import jax.numpy as jnp
from jax import lax
from jax.experimental import pallas as pl
from jax.experimental.pallas import tpu as pltpu
from jax.sharding import PartitionSpec as P

C = 256
EPS = 1e-06
F32 = jnp.float32
BF16 = jnp.bfloat16
PACK = 4 * C + 16
FIRST, SECOND, MIDDLE, LAST = 0, 1, 3, 6


def dot(a, b):
    return jnp.dot(a, b, preferred_element_type=F32)


def dot_t(a, b):
    return lax.dot_general(a, b, (((1,), (1,)), ((), ())), preferred_element_type=F32)


def dot_rows(a, b):
    return lax.dot_general(a, b, (((0,), (0,)), ((), ())), preferred_element_type=F32)


def scale_of(state):
    return lax.rsqrt(jnp.mean(state * state, axis=-1, keepdims=True) + EPS)


def layer_forward(state, gain, first, second):
    normed = (state * scale_of(state) * gain).astype(BF16)
    pre = dot(normed, first)
    act = (pre * jax.nn.sigmoid(pre)).astype(BF16)
    return state + dot(act, second), pre


def layer_backward(grad, state, pre, gain, first, second):
    d_act = dot_t(grad.astype(BF16), second)
    sig = jax.nn.sigmoid(pre)
    slope = sig * (1.0 + pre * (1.0 - sig))
    d_pre = (d_act * slope).astype(BF16)
    d_normed = dot_t(d_pre, first)
    scale = scale_of(state)
    unit = state * scale
    d_unit = d_normed * gain
    inner = jnp.mean(d_unit * unit, axis=-1, keepdims=True)
    return grad + scale * (d_unit - unit * inner)


def position():
    here = lax.axis_index("section")
    return here // 2, here % 2


class Weights:
    def __init__(self, core, refs, packed, sems):
        self.refs, self.packed, self.sems, self.core = refs, packed, sems, core

    def copy(self, ref, slot):
        return pltpu.make_async_copy(ref, self.packed.at[slot], self.sems.at[slot])

    def start(self, pair):
        same, other = self.refs[2 * pair], self.refs[2 * pair + 1]
        self.copy(same, 2 * pair + self.core).start()
        self.copy(other, 2 * pair + 1 - self.core).start()

    def wait(self, slot):
        self.copy(self.refs[0], slot).wait()

    def tail(self, slot):
        return self.packed[slot, 4 * C :].astype(F32)

    def gain(self, slot, layer):
        tail = self.tail(slot)
        return tail[layer : layer + 1] + tail[2 + layer : 3 + layer] + tail[4 + layer : 5 + layer]

    def first(self, slot, layer):
        return self.packed[slot, layer * C : (layer + 1) * C]

    def second(self, slot, layer):
        return self.packed[slot, (2 + layer) * C : (3 + layer) * C]

    def both(self, slot):
        return jnp.max(self.tail(slot)[8:9]) > 1.5

    def forward(self, slot, state, state_ref, pre_ref, out_ref):
        state_ref[slot, 0] = state
        state, pre = layer_forward(state, self.gain(slot, 0), self.first(slot, 0), self.second(slot, 0))
        pre_ref[slot, 0] = pre
        out_ref[slot] = state.astype(BF16)

        @pl.when(self.both(slot))
        def _():
            state_ref[slot, 1] = state
            after, pre = layer_forward(state, self.gain(slot, 1), self.first(slot, 1), self.second(slot, 1))
            pre_ref[slot, 1] = pre
            out_ref[slot] = after.astype(BF16)

    def backward(self, slot, grad, state_ref, pre_ref, grad_ref, kept_from=0):
        grad_ref[...] = grad

        def layer(number):
            return layer_backward(
                grad_ref[...],
                state_ref[slot - kept_from, number],
                pre_ref[slot - kept_from, number],
                self.gain(slot, number),
                self.first(slot, number),
                self.second(slot, number),
            )

        @pl.when(self.both(slot))
        def _():
            grad_ref[...] = layer(1)

        return layer(0).astype(BF16)


def pack_kernel(counts, w_in_ref, w_out_ref, g_ref, packed_ref, tail_ref, sems):
    copies = [
        pltpu.make_async_copy(ref.at[layer], packed_ref.at[pl.ds((2 * side + layer) * C, C)], sems.at[2 * side + layer])
        for side, ref in enumerate((w_in_ref, w_out_ref))
        for layer in range(2)
    ]
    for copy in copies:
        copy.start()
    gains = g_ref[...]
    coarse = gains.astype(BF16).astype(F32)
    rest = gains - coarse
    fine = rest.astype(BF16).astype(F32)
    count = jnp.full((2, C), counts[0].astype(F32))
    rows = [coarse, fine, rest - fine, jnp.zeros_like(coarse), count, jnp.zeros((6, C), F32)]
    tail_ref[...] = jnp.concatenate(rows, 0).astype(BF16)
    copies.append(pltpu.make_async_copy(tail_ref, packed_ref.at[pl.ds(4 * C, 16)], sems.at[4]))
    copies[-1].start()
    for copy in copies:
        copy.wait()


def pair_kernel(chip, x_ref, same, other, outs_ref, skip_ref, rows_same, rows_other, packed, states, pres, sems):
    here, core = position()

    def keep(slot, index, value):
        @pl.when(core == slot)
        def _():
            rows_same[index] = value

        @pl.when(core != slot)
        def _():
            rows_other[index] = value

    @pl.when(here == chip)
    def _():
        weights = Weights(core, [same, other], packed, sems)
        weights.start(0)
        state = (x_ref[core] if chip == FIRST else x_ref[1]).astype(F32)
        for slot in range(2):
            weights.wait(slot)
            weights.forward(slot, state, states, pres, outs_ref)
            keep(slot, 0, outs_ref[slot])
            keep(slot, 1, state.astype(BF16))
            state = outs_ref[slot].astype(F32)
        if chip == SECOND:
            skip_ref[:2] = x_ref[...]
            skip_ref[2:] = outs_ref[...]


def middle_forward_kernel(first_slot, hop_ref, *refs):
    before, refs = (refs[0], refs[1:]) if first_slot else (None, refs)
    pairs = 1 if first_slot else 2
    refs, (outs_ref, inflow_ref, state_ref, pre_ref, packed, sems) = refs[: 2 * pairs], refs[2 * pairs :]
    here, core = position()

    @pl.when(here == MIDDLE)
    def _():
        weights = Weights(core, refs, packed, sems)
        for pair in range(pairs):
            weights.start(pair)
        for slot in range(2 * pairs):
            weights.wait(slot)
            state = (hop_ref[...] if slot == 0 else outs_ref[slot - 1]).astype(F32)
            if first_slot:
                state = state + before[3 - slot].astype(F32)
            inflow_ref[slot] = state.astype(BF16)
            weights.forward(slot, state, state_ref, pre_ref, outs_ref)


def store_by_owner(core, slot, refs, index, value):
    left_same, left_other, right_same, right_other, own_other, own_same = refs
    same, other = ((left_same, left_other), (own_same, own_other), (right_same, right_other))[slot // 2]

    @pl.when(core == slot % 2)
    def _():
        same[index] = value

    @pl.when(core != slot % 2)
    def _():
        other[index] = value


def last_kernel(hop_ref, skip2_ref, skip_ref, ct_ref, outs_low, outs_high, rows_low, rows_high, *refs):
    refs, refs_out = refs[:6], refs[6:]
    owners, (hop_out, sent_out, up_ref) = refs_out[:6], refs_out[6:9]
    packed, outs_ref, inflow_ref, state_ref, pre_ref, sent_ref, grad_ref, sems = refs_out[9:]
    here, core = position()

    def keep_rows(slots, outs, inflows):
        for index, slot in enumerate(slots):
            store_by_owner(core, slot, owners, 0, outs[index])
            store_by_owner(core, slot, owners, 1, inflows[index])

    @pl.when(here == LAST)
    def _():
        weights = Weights(core, refs, packed, sems)
        for pair in range(3):
            weights.start(pair)
        skips = [skip2_ref.at[index] for index in (1, 0)] + [skip_ref.at[index] for index in (3, 2, 1, 0)]
        for slot in range(6):
            weights.wait(slot)
            state = (hop_ref[...] if slot == 0 else outs_ref[slot - 1]).astype(F32)
            state = state + skips[slot][...].astype(F32)
            inflow_ref[slot] = state.astype(BF16)
            weights.forward(slot, state, state_ref, pre_ref, outs_ref)
        for slot in reversed(range(6)):
            up_ref[slot] = ct_ref[core] if slot == 5 else sent_ref[slot + 1]
            grad = up_ref[slot].astype(F32)
            sent_ref[slot] = weights.backward(slot, grad, state_ref, pre_ref, grad_ref)
        hop_out[...] = sent_ref[:2]
        sent_out[...] = sent_ref[2:]
        keep_rows(range(6), outs_ref, inflow_ref)

    @pl.when(here == MIDDLE)
    def _():
        keep_rows(range(4), outs_low, rows_low)
        keep_rows(range(4, 6), outs_high, rows_high)


def middle_backward_kernel(hop_ref, state_low, pre_low, state_high, pre_high, x_ref, *refs):
    refs, low_refs, refs_out = refs[:6], refs[6:10], refs[10:]
    hop_out, up_ref, low_state, low_pre, packed, sent_ref, grad_ref, sems = refs_out
    here, core = position()

    @pl.when(here == SECOND)
    def _():
        weights = Weights(core, low_refs, packed, sems)
        for pair in range(2):
            weights.start(pair)
        for slot in range(4):
            weights.wait(slot)
            state = (x_ref[core] if slot == 0 else sent_ref[slot - 1]).astype(F32)
            weights.forward(slot, state, low_state, low_pre, sent_ref)

    @pl.when(here == MIDDLE)
    def _():
        weights = Weights(core, refs, packed, sems)
        for pair in reversed(range(3)):
            weights.start(pair)
        skips = [hop_ref.at[1], hop_ref.at[0], sent_ref.at[5], sent_ref.at[4]]
        for slot in reversed(range(6)):
            weights.wait(slot)
            grad = (hop_ref[0] if slot == 5 else sent_ref[slot + 1]).astype(F32)
            if slot < 4:
                grad = grad + skips[slot][...].astype(F32)
            up_ref[slot] = grad.astype(BF16)
            if slot < 4:
                sent_ref[slot] = weights.backward(slot, grad, state_low, pre_low, grad_ref)
            else:
                sent_ref[slot] = weights.backward(slot, grad, state_high, pre_high, grad_ref, 4)
        hop_out[...] = sent_ref[0]


def first_backward_kernel(hop_ref, skip_ref, state_ref, pre_ref, up_middle, up_last, *refs):
    rows, refs, refs_out = refs[:6], refs[6:10], refs[10:]
    away, own, (packed, sent_ref, grad_ref, sems, role_sems) = refs_out[:4], refs_out[4:6], refs_out[6:]
    here, core = position()
    owners = list(away) + [ref.at[2] for ref in own]

    def rows_copies(other, same):
        return [
            pltpu.make_async_copy(source, target.at[pl.ds(0, 2)], role_sems.at[number])
            for number, (source, target) in enumerate(zip((other, same), own))
        ]

    for chips, (other, same) in (
        ((here == MIDDLE) | (here == LAST), rows[:2]),
        (here == FIRST, (rows[3], rows[2])),
        (here == SECOND, (rows[5], rows[4])),
    ):

        @pl.when(chips)
        def _():
            for copy in rows_copies(other, same):
                copy.start()

    everything = (slice(None), slice(None))

    @pl.when(here == SECOND)
    def _():
        weights = Weights(core, refs, packed, sems)
        for pair in reversed(range(2)):
            weights.start(pair)
        for slot in reversed(range(4)):
            weights.wait(slot)
            grad = (hop_ref[...] if slot == 3 else sent_ref[slot + 1]).astype(F32)
            grad = grad + skip_ref[3 - slot].astype(F32)
            store_by_owner(core, slot, owners, everything, grad.astype(BF16))
            if slot:
                sent_ref[slot] = weights.backward(slot, grad, state_ref, pre_ref, grad_ref)

    for chip, source in ((MIDDLE, up_middle), (LAST, up_last)):

        @pl.when(here == chip)
        def _():
            for slot in range(6):
                store_by_owner(core, slot, owners, everything, source[slot])

    @pl.when((here <= SECOND) | (here == MIDDLE) | (here == LAST))
    def _():
        for copy in rows_copies(*rows[:2]):
            copy.wait()


def owner_kernel(counts, g_ref, w_in_ref, w_out_ref, *refs):
    pieces, (out_ref, parts_ref, inflow_ref, grad_ref, gw_ref) = refs[:10], refs[10:]
    rows, ups, own = pieces[:4], pieces[4:8], (pieces[9], pieces[8])
    here, core = position()
    pixels = grad_ref.shape[0] // 2
    places = [pl.ds(pl.multiple_of(side * pixels, pixels), pixels) for side in (core, 1 - core)]
    everything = (slice(None), slice(None))

    def take_rows(chips, refs):
        @pl.when(chips)
        def _():
            for ref, side, place in zip(refs, (core, 1 - core), places):
                out_ref[side] = ref[0]
                inflow_ref[place] = ref[1].astype(F32)

    def take_ups(chips, refs, index):
        @pl.when(chips)
        def _():
            for ref, place in zip(refs, places):
                grad_ref[place] = ref[index].astype(F32)

    holds = (here == SECOND) | (here == MIDDLE) | (here == LAST)
    take_rows(holds | (here == FIRST), own)
    take_rows((here == MIDDLE - 1) | (here == LAST - 1), rows[:2])
    take_rows((here == MIDDLE + 1) | (here == LAST + 1), rows[2:])
    take_ups(holds, own, 2)
    take_ups((here == SECOND - 1) | (here == MIDDLE - 1) | (here == LAST - 1), ups[:2], everything)
    take_ups((here == MIDDLE + 1) | (here == LAST + 1), ups[2:], everything)

    inflow = inflow_ref[...]
    after, pre0 = layer_forward(inflow, g_ref[0][None], w_in_ref[0], w_out_ref[0])

    def gradients(layer, state, pre, grad):
        gain = g_ref[layer][None]
        grad_cast = grad.astype(BF16)
        d_act = dot_t(grad_cast, w_out_ref[layer])
        sig = jax.nn.sigmoid(pre)
        act = (pre * sig).astype(BF16)
        d_pre = (d_act * (sig * (1.0 + pre * (1.0 - sig)))).astype(BF16)
        scale = scale_of(state)
        unit = state * scale
        normed = (unit * gain).astype(BF16)
        gw_ref[layer] = dot_rows(normed, d_pre)
        gw_ref[2 + layer] = dot_rows(act, grad_cast)
        return scale, unit, d_pre, gain

    @pl.when(counts[0] > 1)
    def _():
        grad = grad_ref[...]
        pre1 = dot((after * scale_of(after) * g_ref[1][None]).astype(BF16), w_in_ref[1])
        scale, unit, d_pre, gain = gradients(1, after, pre1, grad)
        d_unit = dot_t(d_pre, w_in_ref[1]) * gain
        inner = jnp.mean(d_unit * unit, axis=-1, keepdims=True)
        grad_ref[...] = grad + scale * (d_unit - unit * inner)

    @pl.when(counts[0] <= 1)
    def _():
        gw_ref[1] = jnp.zeros((C, C), F32)
        gw_ref[3] = jnp.zeros((C, C), F32)

    gradients(0, inflow, pre0, grad_ref[...])

    columns, double, _ = parts_ref.shape
    for matrix in range(2):
        both = [gw_ref[2 * matrix + layer].reshape(columns, double // 2, C) for layer in range(2)]
        parts_ref[:, :, matrix * C : (matrix + 1) * C] = jnp.concatenate(both, 1).astype(BF16)


def sum_kernel(parts_ref, w_ref, g_ref, gw_in_ref, gw_out_ref, gain_ref):
    columns, double, _ = parts_ref.shape
    total = parts_ref[0].astype(F32)
    for source in range(1, columns):
        total = total + parts_ref[source].astype(F32)
    share = double // 2
    for layer in range(2):
        rows = total[layer * share : (layer + 1) * share]
        gw_in_ref[layer] = rows[:, :C]
        gw_out_ref[layer] = rows[:, C:]
        product = rows[:, :C] * w_ref[layer]
        ones = jnp.ones((1, C), F32)
        product = lax.dot_general(
            ones, product, (((1,), (1,)), ((), ())), precision=lax.Precision.HIGHEST, preferred_element_type=F32
        )
        gain_ref[layer : layer + 1] = product / g_ref[layer : layer + 1]


def vmem():
    return pl.BlockSpec(memory_space=pltpu.VMEM)


def smem():
    return pl.BlockSpec(memory_space=pltpu.SMEM)


def hbm():
    return pl.BlockSpec(memory_space=pltpu.HBM)


def call(kernel, name, inputs, outputs, scratch=(), us=1, limit=32 * 2**20):
    specs = {"vmem": vmem, "smem": smem, "hbm": hbm}
    outputs = [jax.ShapeDtypeStruct(shape, dtype) for shape, dtype in outputs]
    return pl.pallas_call(
        kernel,
        out_shape=outputs,
        in_specs=[specs[memory]() for memory, _ in inputs],
        out_specs=[vmem() for _ in outputs],
        scratch_shapes=list(scratch),
        compiler_params=pltpu.CompilerParams(vmem_limit_bytes=limit),
        cost_estimate=pl.CostEstimate(flops=us * 10**9, bytes_accessed=2**20, transcendentals=0),
        name=name,
    )(*[array for _, array in inputs])


def at_vmem(*arrays):
    return [("vmem", array) for array in arrays]


def at_hbm(*arrays):
    return [("hbm", array) for array in arrays]


def move(value, chips, cross=False):
    pairs = [(2 * a + core, 2 * b + (1 - core if cross else core)) for a, b in chips for core in range(2)]
    return lax.ppermute(value, "section", pairs)


def packed_scratch(slots):
    return pltpu.VMEM((slots, PACK, C), BF16)


def kept(slots, pixels):
    return pltpu.VMEM((slots, 2, pixels, C), F32)


def body(images, cotangent, w_in, w_out, gains, layer_counts):
    columns = lax.axis_size("dp")
    micro, pixels, _ = images.shape
    tile = (pixels, C)
    dma = pltpu.SemaphoreType.DMA
    barrier = lax.optimization_barrier

    (own,) = call(
        pack_kernel,
        "pack",
        [("smem", layer_counts)] + at_hbm(w_in[0], w_out[0]) + at_vmem(gains[0]),
        [((PACK, C), BF16)],
        [pltpu.VMEM((16, C), BF16), dma((5,))],
    )
    holders = (MIDDLE, LAST)
    low_own = move(own, [(chip, chip) for chip in (FIRST, SECOND)], cross=True)
    left = move(own, [(chip - 1, chip) for chip in holders])
    right = move(own, [(chip + 1, chip) for chip in holders])

    def pair(chip, value):
        return call(
            lambda *refs: pair_kernel(chip, *refs),
            "pair_forward",
            at_vmem(value) + at_hbm(own, low_own),
            [((2,) + tile, BF16), ((4,) + tile, BF16)] + [((2,) + tile, BF16)] * 2,
            [packed_scratch(2), kept(2, pixels), kept(2, pixels), dma((2,))],
        )

    outs_a, _, *rows_a = pair(FIRST, images)
    outs_b, skip, *rows_b = pair(SECOND, move(outs_a, [(FIRST, SECOND)]))
    hop = move(outs_b[1], [(SECOND, MIDDLE)])
    partner = move(barrier((own, low_own))[0], [(chip, chip) for chip in holders], cross=True)
    left, right, later, partner, hop = barrier((left, right, own, partner, hop))
    left_partner = move(left, [(chip, chip) for chip in holders], cross=True)
    right_partner = move(right, [(chip, chip) for chip in holders], cross=True)
    weights = at_hbm(left, left_partner, own, partner, right, right_partner)
    four, six, four_state = (4,) + tile, (6,) + tile, (4, 2) + tile

    def middle(first_slot, slots, value, refs):
        slots, state_shape = (slots,) + tile, (slots, 2) + tile
        return call(
            functools.partial(middle_forward_kernel, first_slot),
            "middle_forward",
            at_vmem(*value) + refs,
            [(slots, BF16), (slots, BF16), (state_shape, F32), (state_shape, F32)],
            [packed_scratch(slots[0]), dma((slots[0],))],
            us=slots[0] // 2,
        )

    outs_low, *kept_low = middle(0, 4, [hop], weights[:4])
    outs_high, *kept_high = middle(4, 2, [outs_low[3], outs_low], weights[4:])
    skip2 = move(outs_low[:2], [(MIDDLE, LAST)])
    hop = outs_high[1]
    skip, hop = barrier((skip, hop))
    hop = move(hop, [(MIDDLE, LAST)])
    skip = move(skip, [(SECOND, LAST)])
    low_left = move(later, [(SECOND - 1, SECOND)])
    low_partner = move(low_left, [(SECOND, SECOND)], cross=True)
    low_weights = at_hbm(low_left, low_partner, own, low_own)
    *to_owners, hop, skips, ups_last = call(
        last_kernel,
        "last_both",
        at_vmem(hop, skip2, skip, cotangent, outs_low, outs_high, kept_low[0], kept_high[0]) + weights,
        [((2,) + tile, BF16)] * 6 + [((2,) + tile, BF16), (four, BF16), (six, BF16)],
        [
            packed_scratch(6),
            pltpu.VMEM(six, BF16),
            pltpu.VMEM(six, BF16),
            kept(6, pixels),
            kept(6, pixels),
            pltpu.VMEM(six, BF16),
            pltpu.VMEM(tile, F32),
            dma((6,)),
        ],
        us=8,
    )
    hop = move(hop, [(LAST, MIDDLE)])
    skips = move(skips, [(LAST, SECOND)])

    def deliver(chips, *pieces):
        lefts = [(chip, chip - 1) for chip in chips]
        rights = [(chip, chip + 1) for chip in (MIDDLE, LAST)]
        routes = ((lefts, False), (lefts, True), (rights, False), (rights, True))
        return [move(piece, *route) for piece, route in zip(pieces, routes) if piece is not None]

    *away, rows_other, rows_same = to_owners
    rows_left, rows_right = away[:2], deliver((MIDDLE, LAST), None, None, *away[2:])
    hop, rows_right = barrier((hop, rows_right))
    hop, ups_middle, low_states, low_pres = call(
        middle_backward_kernel,
        "middle_backward",
        at_vmem(hop, *kept_low[1:], *kept_high[1:], images) + weights + low_weights,
        [(tile, BF16), (six, BF16), (four_state, F32), (four_state, F32)],
        [packed_scratch(6), pltpu.VMEM(six, BF16), pltpu.VMEM(tile, F32), dma((6,))],
        us=5,
    )
    rows_left, hop = barrier((rows_left, hop))
    hop = move(hop, [(MIDDLE, SECOND)])
    rows = deliver((MIDDLE, LAST), *rows_left) + rows_right
    *away, own_other, own_same = call(
        first_backward_kernel,
        "first_backward",
        at_vmem(hop, skips, low_states, low_pres, ups_middle, ups_last)
        + at_hbm(rows_other, rows_same, *rows_a, *rows_b)
        + low_weights,
        [(tile, BF16)] * 4 + [((3,) + tile, BF16)] * 2,
        [packed_scratch(4), pltpu.VMEM(four, BF16), pltpu.VMEM(tile, F32), dma((4,)), dma((2,))],
        us=3,
    )
    ups = deliver((SECOND, MIDDLE, LAST), *away)
    own_other = move(own_other, [(chip, chip) for chip in (FIRST, SECOND, MIDDLE, LAST)], cross=True)

    share = C // columns
    section_outputs, parts = call(
        owner_kernel,
        "owner_gradients",
        [("smem", layer_counts)] + at_vmem(gains[0], w_in[0], w_out[0], *rows, *ups, own_other, own_same),
        [((micro, pixels, C), BF16), ((columns, 2 * share, 2 * C), BF16)],
        [pltpu.VMEM((micro * pixels, C), F32)] * 2 + [pltpu.VMEM((4, C, C), F32)],
    )
    parts = lax.all_to_all(parts, "dp", 0, 0, tiled=True)
    start = lax.axis_index("dp") * share
    w_rows = lax.dynamic_slice_in_dim(w_in[0], start, share, 1).astype(F32)
    gain_rows = lax.dynamic_slice_in_dim(gains[0], start, share, 1)
    grad_in, grad_out, grad_gain = call(
        sum_kernel,
        "sum_parts",
        at_vmem(parts, w_rows, gain_rows),
        [((2, share, C), F32), ((2, share, C), F32), ((2, share), F32)],
    )
    return section_outputs[None], grad_in[None], grad_out[None], grad_gain[None]


def solution(mesh):
    return jax.shard_map(
        body,
        mesh=mesh,
        in_specs=(
            P(None, "dp", None),
            P(None, "dp", None),
            P("section", None, None, None),
            P("section", None, None, None),
            P("section", None, None),
            P("section"),
        ),
        out_specs=(
            P("section", None, "dp", None),
            P("section", None, "dp", None),
            P("section", None, "dp", None),
            P("section", None, "dp"),
        ),
        check_vma=False,
    )
```

```python
import functools

import jax
import jax.numpy as jnp
from jax import lax
from jax.experimental import pallas as pl
from jax.experimental.pallas import tpu as pltpu
from jax.sharding import PartitionSpec as P

C = 256
EPS = 1e-06
F32 = jnp.float32
BF16 = jnp.bfloat16
PACK = 4 * C + 16
FIRST, SECOND, MIDDLE, LAST = 0, 1, 3, 6


def dot(a, b):
    return jnp.dot(a, b, preferred_element_type=F32)


def dot_t(a, b):
    return lax.dot_general(a, b, (((1,), (1,)), ((), ())), preferred_element_type=F32)


def dot_rows(a, b):
    return lax.dot_general(a, b, (((0,), (0,)), ((), ())), preferred_element_type=F32)


def scale_of(state):
    return lax.rsqrt(jnp.mean(state * state, axis=-1, keepdims=True) + EPS)


def layer_forward(state, gain, first, second):
    normed = (state * scale_of(state) * gain).astype(BF16)
    pre = dot(normed, first)
    act = (pre * jax.nn.sigmoid(pre)).astype(BF16)
    return state + dot(act, second), pre


def layer_backward(grad, state, pre, gain, first, second):
    d_act = dot_t(grad.astype(BF16), second)
    sig = jax.nn.sigmoid(pre)
    slope = sig * (1.0 + pre * (1.0 - sig))
    d_pre = (d_act * slope).astype(BF16)
    d_normed = dot_t(d_pre, first)
    scale = scale_of(state)
    unit = state * scale
    d_unit = d_normed * gain
    inner = jnp.mean(d_unit * unit, axis=-1, keepdims=True)
    return grad + scale * (d_unit - unit * inner)


def position():
    here = lax.axis_index("section")
    return here // 2, here % 2


class Weights:
    def __init__(self, core, refs, packed, sems):
        self.refs, self.packed, self.sems, self.core = refs, packed, sems, core

    def copy(self, ref, slot):
        return pltpu.make_async_copy(ref, self.packed.at[slot], self.sems.at[slot])

    def start(self, pair):
        same, other = self.refs[2 * pair], self.refs[2 * pair + 1]
        self.copy(same, 2 * pair + self.core).start()
        self.copy(other, 2 * pair + 1 - self.core).start()

    def wait(self, slot):
        self.copy(self.refs[0], slot).wait()

    def tail(self, slot):
        return self.packed[slot, 4 * C :].astype(F32)

    def gain(self, slot, layer):
        tail = self.tail(slot)
        return tail[layer : layer + 1] + tail[2 + layer : 3 + layer] + tail[4 + layer : 5 + layer]

    def first(self, slot, layer):
        return self.packed[slot, layer * C : (layer + 1) * C]

    def second(self, slot, layer):
        return self.packed[slot, (2 + layer) * C : (3 + layer) * C]

    def both(self, slot):
        return jnp.max(self.tail(slot)[8:9]) > 1.5

    def forward(self, slot, state, state_ref, pre_ref, out_ref):
        state_ref[slot, 0] = state
        state, pre = layer_forward(state, self.gain(slot, 0), self.first(slot, 0), self.second(slot, 0))
        pre_ref[slot, 0] = pre
        out_ref[slot] = state.astype(BF16)

        @pl.when(self.both(slot))
        def _():
            state_ref[slot, 1] = state
            after, pre = layer_forward(state, self.gain(slot, 1), self.first(slot, 1), self.second(slot, 1))
            pre_ref[slot, 1] = pre
            out_ref[slot] = after.astype(BF16)

    def backward(self, slot, grad, state_ref, pre_ref, grad_ref, kept_from=0):
        grad_ref[...] = grad

        def layer(number):
            return layer_backward(
                grad_ref[...],
                state_ref[slot - kept_from, number],
                pre_ref[slot - kept_from, number],
                self.gain(slot, number),
                self.first(slot, number),
                self.second(slot, number),
            )

        @pl.when(self.both(slot))
        def _():
            grad_ref[...] = layer(1)

        return layer(0).astype(BF16)


def pack_kernel(counts, w_in_ref, w_out_ref, g_ref, packed_ref, gains_ref, sems):
    copies = [
        pltpu.make_async_copy(
            ref.at[layer, pl.ds(part * C // 2, C // 2)],
            packed_ref.at[pl.ds((2 * side + layer) * C + part * C // 2, C // 2)],
            sems.at[4 * side + 2 * layer + part],
        )
        for side, ref in enumerate((w_in_ref, w_out_ref))
        for layer in range(2)
        for part in range(2)
    ]
    gains_copy = pltpu.make_async_copy(g_ref, gains_ref, sems.at[8])
    gains_copy.start()
    for copy in copies:
        copy.start()
    gains_copy.wait()
    gains = gains_ref[...]
    coarse = gains.astype(BF16).astype(F32)
    rest = gains - coarse
    fine = rest.astype(BF16).astype(F32)
    count = jnp.full((2, C), counts[0].astype(F32))
    rows = [coarse, fine, rest - fine, jnp.zeros_like(coarse), count, jnp.zeros((6, C), F32)]
    packed_ref[4 * C :] = jnp.concatenate(rows, 0).astype(BF16)
    for copy in copies:
        copy.wait()


def pair_kernel(chip, x_ref, same, other, outs_ref, skip_ref, rows_same, rows_other, packed, states, pres, sems):
    here, core = position()

    def keep(slot, index, value):
        @pl.when(core == slot)
        def _():
            rows_same[index] = value

        @pl.when(core != slot)
        def _():
            rows_other[index] = value

    @pl.when(here == chip)
    def _():
        weights = Weights(core, [same, other], packed, sems)
        weights.start(0)
        state = (x_ref[core] if chip == FIRST else x_ref[1]).astype(F32)
        for slot in range(2):
            weights.wait(slot)
            weights.forward(slot, state, states, pres, outs_ref)
            keep(slot, 0, outs_ref[slot])
            keep(slot, 1, state.astype(BF16))
            state = outs_ref[slot].astype(F32)
        if chip == SECOND:
            skip_ref[:2] = x_ref[...]
            skip_ref[2:] = outs_ref[...]


def middle_forward_kernel(first_slot, hop_ref, *refs):
    before, refs = (refs[0], refs[1:]) if first_slot else (None, refs)
    pairs = 1 if first_slot else 2
    refs, (outs_ref, inflow_ref, state_ref, pre_ref, packed, sems) = refs[: 2 * pairs], refs[2 * pairs :]
    here, core = position()

    @pl.when(here == MIDDLE)
    def _():
        weights = Weights(core, refs, packed, sems)
        for pair in range(pairs):
            weights.start(pair)
        for slot in range(2 * pairs):
            weights.wait(slot)
            state = (hop_ref[...] if slot == 0 else outs_ref[slot - 1]).astype(F32)
            if first_slot:
                state = state + before[3 - slot].astype(F32)
            inflow_ref[slot] = state.astype(BF16)
            weights.forward(slot, state, state_ref, pre_ref, outs_ref)


def store_by_owner(core, slot, refs, index, value):
    left_same, left_other, right_same, right_other, own_other, own_same = refs
    same, other = ((left_same, left_other), (own_same, own_other), (right_same, right_other))[slot // 2]

    @pl.when(core == slot % 2)
    def _():
        same[index] = value

    @pl.when(core != slot % 2)
    def _():
        other[index] = value


def last_kernel(hop_ref, skip2_ref, skip_ref, ct_ref, outs_low, outs_high, rows_low, rows_high, *refs):
    refs, refs_out = refs[:6], refs[6:]
    owners, (hop_out, sent_out, up_ref) = refs_out[:6], refs_out[6:9]
    packed, outs_ref, inflow_ref, state_ref, pre_ref, sent_ref, grad_ref, sems = refs_out[9:]
    here, core = position()

    def keep_rows(slots, outs, inflows):
        for index, slot in enumerate(slots):
            store_by_owner(core, slot, owners, 0, outs[index])
            store_by_owner(core, slot, owners, 1, inflows[index])

    @pl.when(here == LAST)
    def _():
        weights = Weights(core, refs, packed, sems)
        for pair in range(3):
            weights.start(pair)
        skips = [skip2_ref.at[index] for index in (1, 0)] + [skip_ref.at[index] for index in (3, 2, 1, 0)]
        for slot in range(6):
            weights.wait(slot)
            state = (hop_ref[...] if slot == 0 else outs_ref[slot - 1]).astype(F32)
            state = state + skips[slot][...].astype(F32)
            inflow_ref[slot] = state.astype(BF16)
            weights.forward(slot, state, state_ref, pre_ref, outs_ref)
        for slot in reversed(range(6)):
            up_ref[slot] = ct_ref[core] if slot == 5 else sent_ref[slot + 1]
            grad = up_ref[slot].astype(F32)
            sent_ref[slot] = weights.backward(slot, grad, state_ref, pre_ref, grad_ref)
        hop_out[...] = sent_ref[:2]
        sent_out[...] = sent_ref[2:]
        keep_rows(range(6), outs_ref, inflow_ref)

    @pl.when(here == MIDDLE)
    def _():
        keep_rows(range(4), outs_low, rows_low)
        keep_rows(range(4, 6), outs_high, rows_high)


def middle_backward_kernel(hop_ref, state_low, pre_low, state_high, pre_high, x_ref, *refs):
    refs, low_refs, refs_out = refs[:6], refs[6:10], refs[10:]
    hop_out, up_ref, low_state, low_pre, packed, sent_ref, grad_ref, sems = refs_out
    here, core = position()

    @pl.when(here == SECOND)
    def _():
        weights = Weights(core, low_refs, packed, sems)
        for pair in range(2):
            weights.start(pair)
        for slot in range(4):
            weights.wait(slot)
            state = (x_ref[core] if slot == 0 else sent_ref[slot - 1]).astype(F32)
            weights.forward(slot, state, low_state, low_pre, sent_ref)

    @pl.when(here == MIDDLE)
    def _():
        weights = Weights(core, refs, packed, sems)
        for pair in reversed(range(3)):
            weights.start(pair)
        skips = [hop_ref.at[1], hop_ref.at[0], sent_ref.at[5], sent_ref.at[4]]
        for slot in reversed(range(6)):
            weights.wait(slot)
            grad = (hop_ref[0] if slot == 5 else sent_ref[slot + 1]).astype(F32)
            if slot < 4:
                grad = grad + skips[slot][...].astype(F32)
            up_ref[slot] = grad.astype(BF16)
            if slot < 4:
                sent_ref[slot] = weights.backward(slot, grad, state_low, pre_low, grad_ref)
            else:
                sent_ref[slot] = weights.backward(slot, grad, state_high, pre_high, grad_ref, 4)
        hop_out[...] = sent_ref[0]


def first_backward_kernel(hop_ref, skip_ref, state_ref, pre_ref, up_middle, up_last, *refs):
    rows, refs, refs_out = refs[:6], refs[6:10], refs[10:]
    away, own, (packed, sent_ref, grad_ref, sems, role_sems) = refs_out[:4], refs_out[4:6], refs_out[6:]
    here, core = position()
    owners = list(away) + [ref.at[2] for ref in own]

    def rows_copies(other, same):
        return [
            pltpu.make_async_copy(source, target.at[pl.ds(0, 2)], role_sems.at[number])
            for number, (source, target) in enumerate(zip((other, same), own))
        ]

    for chips, (other, same) in (
        ((here == MIDDLE) | (here == LAST), rows[:2]),
        (here == FIRST, (rows[3], rows[2])),
        (here == SECOND, (rows[5], rows[4])),
    ):

        @pl.when(chips)
        def _():
            for copy in rows_copies(other, same):
                copy.start()

    everything = (slice(None), slice(None))

    @pl.when(here == SECOND)
    def _():
        weights = Weights(core, refs, packed, sems)
        for pair in reversed(range(2)):
            weights.start(pair)
        for slot in reversed(range(4)):
            weights.wait(slot)
            grad = (hop_ref[...] if slot == 3 else sent_ref[slot + 1]).astype(F32)
            grad = grad + skip_ref[3 - slot].astype(F32)
            store_by_owner(core, slot, owners, everything, grad.astype(BF16))
            if slot:
                sent_ref[slot] = weights.backward(slot, grad, state_ref, pre_ref, grad_ref)

    for chip, source in ((MIDDLE, up_middle), (LAST, up_last)):

        @pl.when(here == chip)
        def _():
            for slot in range(6):
                store_by_owner(core, slot, owners, everything, source[slot])

    @pl.when((here <= SECOND) | (here == MIDDLE) | (here == LAST))
    def _():
        for copy in rows_copies(*rows[:2]):
            copy.wait()


def owner_kernel(counts, g_ref, w_in_ref, w_out_ref, *refs):
    pieces, (out_ref, parts_ref, inflow_ref, grad_ref, gw_ref) = refs[:10], refs[10:]
    rows, ups, own = pieces[:4], pieces[4:8], (pieces[9], pieces[8])
    here, core = position()
    pixels = grad_ref.shape[0] // 2
    places = [pl.ds(pl.multiple_of(side * pixels, pixels), pixels) for side in (core, 1 - core)]
    everything = (slice(None), slice(None))

    def take_rows(chips, refs):
        @pl.when(chips)
        def _():
            for ref, side, place in zip(refs, (core, 1 - core), places):
                out_ref[side] = ref[0]
                inflow_ref[place] = ref[1].astype(F32)

    def take_ups(chips, refs, index):
        @pl.when(chips)
        def _():
            for ref, place in zip(refs, places):
                grad_ref[place] = ref[index].astype(F32)

    holds = (here == SECOND) | (here == MIDDLE) | (here == LAST)
    take_rows(holds | (here == FIRST), own)
    take_rows((here == MIDDLE - 1) | (here == LAST - 1), rows[:2])
    take_rows((here == MIDDLE + 1) | (here == LAST + 1), rows[2:])
    take_ups(holds, own, 2)
    take_ups((here == SECOND - 1) | (here == MIDDLE - 1) | (here == LAST - 1), ups[:2], everything)
    take_ups((here == MIDDLE + 1) | (here == LAST + 1), ups[2:], everything)

    inflow = inflow_ref[...]
    after, pre0 = layer_forward(inflow, g_ref[0][None], w_in_ref[0], w_out_ref[0])

    def gradients(layer, state, pre, grad):
        gain = g_ref[layer][None]
        grad_cast = grad.astype(BF16)
        d_act = dot_t(grad_cast, w_out_ref[layer])
        sig = jax.nn.sigmoid(pre)
        act = (pre * sig).astype(BF16)
        d_pre = (d_act * (sig * (1.0 + pre * (1.0 - sig)))).astype(BF16)
        scale = scale_of(state)
        unit = state * scale
        normed = (unit * gain).astype(BF16)
        gw_ref[layer] = dot_rows(normed, d_pre)
        gw_ref[2 + layer] = dot_rows(act, grad_cast)
        return scale, unit, d_pre, gain

    @pl.when(counts[0] > 1)
    def _():
        grad = grad_ref[...]
        pre1 = dot((after * scale_of(after) * g_ref[1][None]).astype(BF16), w_in_ref[1])
        scale, unit, d_pre, gain = gradients(1, after, pre1, grad)
        d_unit = dot_t(d_pre, w_in_ref[1]) * gain
        inner = jnp.mean(d_unit * unit, axis=-1, keepdims=True)
        grad_ref[...] = grad + scale * (d_unit - unit * inner)

    @pl.when(counts[0] <= 1)
    def _():
        gw_ref[1] = jnp.zeros((C, C), F32)
        gw_ref[3] = jnp.zeros((C, C), F32)

    gradients(0, inflow, pre0, grad_ref[...])

    columns, double, _ = parts_ref.shape
    for matrix in range(2):
        both = [gw_ref[2 * matrix + layer].reshape(columns, double // 2, C) for layer in range(2)]
        parts_ref[:, :, matrix * C : (matrix + 1) * C] = jnp.concatenate(both, 1).astype(BF16)


def sum_kernel(parts_ref, w_ref, g_ref, gw_in_ref, gw_out_ref, gain_ref):
    columns, double, _ = parts_ref.shape
    total = parts_ref[0].astype(F32)
    for source in range(1, columns):
        total = total + parts_ref[source].astype(F32)
    share = double // 2
    for layer in range(2):
        rows = total[layer * share : (layer + 1) * share]
        gw_in_ref[layer] = rows[:, :C]
        gw_out_ref[layer] = rows[:, C:]
        product = rows[:, :C] * w_ref[layer]
        ones = jnp.ones((1, C), F32)
        product = lax.dot_general(
            ones, product, (((1,), (1,)), ((), ())), precision=lax.Precision.HIGHEST, preferred_element_type=F32
        )
        gain_ref[layer : layer + 1] = product / g_ref[layer : layer + 1]


def vmem():
    return pl.BlockSpec(memory_space=pltpu.VMEM)


def smem():
    return pl.BlockSpec(memory_space=pltpu.SMEM)


def hbm():
    return pl.BlockSpec(memory_space=pltpu.HBM)


def call(kernel, name, inputs, outputs, scratch=(), us=1, limit=32 * 2**20):
    specs = {"vmem": vmem, "smem": smem, "hbm": hbm}
    outputs = [jax.ShapeDtypeStruct(shape, dtype) for shape, dtype in outputs]
    return pl.pallas_call(
        kernel,
        out_shape=outputs,
        in_specs=[specs[memory]() for memory, _ in inputs],
        out_specs=[vmem() for _ in outputs],
        scratch_shapes=list(scratch),
        compiler_params=pltpu.CompilerParams(vmem_limit_bytes=limit),
        cost_estimate=pl.CostEstimate(flops=us * 10**9, bytes_accessed=2**20, transcendentals=0),
        name=name,
    )(*[array for _, array in inputs])


def at_vmem(*arrays):
    return [("vmem", array) for array in arrays]


def at_hbm(*arrays):
    return [("hbm", array) for array in arrays]


def move(value, chips, cross=False):
    pairs = [(2 * a + core, 2 * b + (1 - core if cross else core)) for a, b in chips for core in range(2)]
    return lax.ppermute(value, "section", pairs)


def packed_scratch(slots):
    return pltpu.VMEM((slots, PACK, C), BF16)


def kept(slots, pixels):
    return pltpu.VMEM((slots, 2, pixels, C), F32)


def body(images, cotangent, w_in, w_out, gains, layer_counts):
    columns = lax.axis_size("dp")
    micro, pixels, _ = images.shape
    tile = (pixels, C)
    dma = pltpu.SemaphoreType.DMA
    barrier = lax.optimization_barrier

    (own,) = call(
        pack_kernel,
        "pack",
        [("smem", layer_counts)] + at_hbm(w_in[0], w_out[0], gains[0]),
        [((PACK, C), BF16)],
        [pltpu.VMEM((2, C), F32), dma((9,))],
        limit=62600000,
    )
    holders = (MIDDLE, LAST)
    low_own = move(own, [(chip, chip) for chip in (FIRST, SECOND)], cross=True)
    left = move(own, [(chip - 1, chip) for chip in holders])
    right = move(own, [(chip + 1, chip) for chip in holders])

    def pair(chip, value):
        return call(
            lambda *refs: pair_kernel(chip, *refs),
            "pair_forward",
            at_vmem(value) + at_hbm(own, low_own),
            [((2,) + tile, BF16), ((4,) + tile, BF16)] + [((2,) + tile, BF16)] * 2,
            [packed_scratch(2), kept(2, pixels), kept(2, pixels), dma((2,))],
        )

    outs_a, _, *rows_a = pair(FIRST, images)
    outs_b, skip, *rows_b = pair(SECOND, move(outs_a, [(FIRST, SECOND)]))
    hop = move(outs_b[1], [(SECOND, MIDDLE)])
    partner = move(barrier((own, low_own))[0], [(chip, chip) for chip in holders], cross=True)
    left, right, later, partner, hop = barrier((left, right, own, partner, hop))
    left_partner = move(left, [(chip, chip) for chip in holders], cross=True)
    right_partner = move(right, [(chip, chip) for chip in holders], cross=True)
    weights = at_hbm(left, left_partner, own, partner, right, right_partner)
    four, six, four_state = (4,) + tile, (6,) + tile, (4, 2) + tile

    def middle(first_slot, slots, value, refs):
        slots, state_shape = (slots,) + tile, (slots, 2) + tile
        return call(
            functools.partial(middle_forward_kernel, first_slot),
            "middle_forward",
            at_vmem(*value) + refs,
            [(slots, BF16), (slots, BF16), (state_shape, F32), (state_shape, F32)],
            [packed_scratch(slots[0]), dma((slots[0],))],
            us=slots[0] // 2,
        )

    outs_low, *kept_low = middle(0, 4, [hop], weights[:4])
    outs_high, *kept_high = middle(4, 2, [outs_low[3], outs_low], weights[4:])
    skip2 = move(outs_low[:2], [(MIDDLE, LAST)])
    hop = outs_high[1]
    skip, hop = barrier((skip, hop))
    hop = move(hop, [(MIDDLE, LAST)])
    skip = move(skip, [(SECOND, LAST)])
    low_left = move(later, [(SECOND - 1, SECOND)])
    low_partner = move(low_left, [(SECOND, SECOND)], cross=True)
    low_weights = at_hbm(low_left, low_partner, own, low_own)
    *to_owners, hop, skips, ups_last = call(
        last_kernel,
        "last_both",
        at_vmem(hop, skip2, skip, cotangent, outs_low, outs_high, kept_low[0], kept_high[0]) + weights,
        [((2,) + tile, BF16)] * 6 + [((2,) + tile, BF16), (four, BF16), (six, BF16)],
        [
            packed_scratch(6),
            pltpu.VMEM(six, BF16),
            pltpu.VMEM(six, BF16),
            kept(6, pixels),
            kept(6, pixels),
            pltpu.VMEM(six, BF16),
            pltpu.VMEM(tile, F32),
            dma((6,)),
        ],
        us=8,
    )
    hop = move(hop, [(LAST, MIDDLE)])
    skips = move(skips, [(LAST, SECOND)])

    def deliver(chips, *pieces):
        lefts = [(chip, chip - 1) for chip in chips]
        rights = [(chip, chip + 1) for chip in (MIDDLE, LAST)]
        routes = ((lefts, False), (lefts, True), (rights, False), (rights, True))
        return [move(piece, *route) for piece, route in zip(pieces, routes) if piece is not None]

    *away, rows_other, rows_same = to_owners
    rows_left, rows_right = away[:2], deliver((MIDDLE, LAST), None, None, *away[2:])
    hop, rows_right = barrier((hop, rows_right))
    hop, ups_middle, low_states, low_pres = call(
        middle_backward_kernel,
        "middle_backward",
        at_vmem(hop, *kept_low[1:], *kept_high[1:], images) + weights + low_weights,
        [(tile, BF16), (six, BF16), (four_state, F32), (four_state, F32)],
        [packed_scratch(6), pltpu.VMEM(six, BF16), pltpu.VMEM(tile, F32), dma((6,))],
        us=5,
    )
    rows_left, hop = barrier((rows_left, hop))
    hop = move(hop, [(MIDDLE, SECOND)])
    rows = deliver((MIDDLE, LAST), *rows_left) + rows_right
    *away, own_other, own_same = call(
        first_backward_kernel,
        "first_backward",
        at_vmem(hop, skips, low_states, low_pres, ups_middle, ups_last)
        + at_hbm(rows_other, rows_same, *rows_a, *rows_b)
        + low_weights,
        [(tile, BF16)] * 4 + [((3,) + tile, BF16)] * 2,
        [packed_scratch(4), pltpu.VMEM(four, BF16), pltpu.VMEM(tile, F32), dma((4,)), dma((2,))],
        us=3,
    )
    ups = deliver((SECOND, MIDDLE, LAST), *away)
    own_other = move(own_other, [(chip, chip) for chip in (FIRST, SECOND, MIDDLE, LAST)], cross=True)

    share = C // columns
    section_outputs, parts = call(
        owner_kernel,
        "owner_gradients",
        [("smem", layer_counts)] + at_vmem(gains[0], w_in[0], w_out[0], *rows, *ups, own_other, own_same),
        [((micro, pixels, C), BF16), ((columns, 2 * share, 2 * C), BF16)],
        [pltpu.VMEM((micro * pixels, C), F32)] * 2 + [pltpu.VMEM((4, C, C), F32)],
    )
    parts = lax.all_to_all(parts, "dp", 0, 0, tiled=True)
    start = lax.axis_index("dp") * share
    w_rows = lax.dynamic_slice_in_dim(w_in[0], start, share, 1).astype(F32)
    gain_rows = lax.dynamic_slice_in_dim(gains[0], start, share, 1)
    grad_in, grad_out, grad_gain = call(
        sum_kernel,
        "sum_parts",
        at_vmem(parts, w_rows, gain_rows),
        [((2, share, C), F32), ((2, share, C), F32), ((2, share), F32)],
    )
    return section_outputs[None], grad_in[None], grad_out[None], grad_gain[None]


def solution(mesh):
    return jax.shard_map(
        body,
        mesh=mesh,
        in_specs=(
            P(None, "dp", None),
            P(None, "dp", None),
            P("section", None, None, None),
            P("section", None, None, None),
            P("section", None, None),
            P("section"),
        ),
        out_specs=(
            P("section", None, "dp", None),
            P("section", None, "dp", None),
            P("section", None, "dp", None),
            P("section", None, "dp"),
        ),
        check_vma=False,
    )
```

```python
import functools

import jax
import jax.numpy as jnp
from jax import lax
from jax.experimental import pallas as pl
from jax.experimental.pallas import tpu as pltpu
from jax.sharding import PartitionSpec as P

C = 256
EPS = 1e-06
F32 = jnp.float32
BF16 = jnp.bfloat16
PACK = 4 * C + 16
FIRST, SECOND, MIDDLE, LAST = 0, 1, 3, 6


def dot(a, b):
    return jnp.dot(a, b, preferred_element_type=F32)


def dot_t(a, b):
    return lax.dot_general(a, b, (((1,), (1,)), ((), ())), preferred_element_type=F32)


def dot_rows(a, b):
    return lax.dot_general(a, b, (((0,), (0,)), ((), ())), preferred_element_type=F32)


def scale_of(state):
    return lax.rsqrt(jnp.mean(state * state, axis=-1, keepdims=True) + EPS)


def layer_forward(state, gain, first, second):
    normed = (state * scale_of(state) * gain).astype(BF16)
    pre = dot(normed, first)
    act = (pre * jax.nn.sigmoid(pre)).astype(BF16)
    return state + dot(act, second), pre


def layer_backward(grad, state, pre, gain, first, second):
    d_act = dot_t(grad.astype(BF16), second)
    sig = jax.nn.sigmoid(pre)
    slope = sig * (1.0 + pre * (1.0 - sig))
    d_pre = (d_act * slope).astype(BF16)
    d_normed = dot_t(d_pre, first)
    scale = scale_of(state)
    unit = state * scale
    d_unit = d_normed * gain
    inner = jnp.mean(d_unit * unit, axis=-1, keepdims=True)
    return grad + scale * (d_unit - unit * inner)


def position():
    here = lax.axis_index("section")
    return here // 2, here % 2


class Weights:
    def __init__(self, core, refs, packed, sems):
        self.refs, self.packed, self.sems, self.core = refs, packed, sems, core

    def copy(self, ref, slot):
        return pltpu.make_async_copy(ref, self.packed.at[slot], self.sems.at[slot])

    def start(self, pair):
        same, other = self.refs[2 * pair], self.refs[2 * pair + 1]
        self.copy(same, 2 * pair + self.core).start()
        self.copy(other, 2 * pair + 1 - self.core).start()

    def wait(self, slot):
        self.copy(self.refs[0], slot).wait()

    def tail(self, slot):
        return self.packed[slot, 4 * C :].astype(F32)

    def gain(self, slot, layer):
        tail = self.tail(slot)
        return tail[layer : layer + 1] + tail[2 + layer : 3 + layer] + tail[4 + layer : 5 + layer]

    def first(self, slot, layer):
        return self.packed[slot, layer * C : (layer + 1) * C]

    def second(self, slot, layer):
        return self.packed[slot, (2 + layer) * C : (3 + layer) * C]

    def both(self, slot):
        return jnp.max(self.tail(slot)[8:9]) > 1.5

    def forward(self, slot, state, state_ref, pre_ref, out_ref):
        state_ref[slot, 0] = state
        state, pre = layer_forward(state, self.gain(slot, 0), self.first(slot, 0), self.second(slot, 0))
        pre_ref[slot, 0] = pre
        out_ref[slot] = state.astype(BF16)

        @pl.when(self.both(slot))
        def _():
            state_ref[slot, 1] = state
            after, pre = layer_forward(state, self.gain(slot, 1), self.first(slot, 1), self.second(slot, 1))
            pre_ref[slot, 1] = pre
            out_ref[slot] = after.astype(BF16)

    def backward(self, slot, grad, state_ref, pre_ref, grad_ref):
        grad_ref[...] = grad

        def layer(number):
            return layer_backward(
                grad_ref[...],
                state_ref[slot, number],
                pre_ref[slot, number],
                self.gain(slot, number),
                self.first(slot, number),
                self.second(slot, number),
            )

        @pl.when(self.both(slot))
        def _():
            grad_ref[...] = layer(1)

        return layer(0).astype(BF16)


def pack_kernel(counts, w_in_ref, w_out_ref, g_ref, packed_ref, gains_ref, sems):
    copies = [
        pltpu.make_async_copy(
            ref.at[layer, pl.ds(part * C // 2, C // 2)],
            packed_ref.at[pl.ds((2 * side + layer) * C + part * C // 2, C // 2)],
            sems.at[4 * side + 2 * layer + part],
        )
        for side, ref in enumerate((w_in_ref, w_out_ref))
        for layer in range(2)
        for part in range(2)
    ]
    gains_copy = pltpu.make_async_copy(g_ref, gains_ref, sems.at[8])
    gains_copy.start()
    for copy in copies:
        copy.start()
    gains_copy.wait()
    gains = gains_ref[...]
    coarse = gains.astype(BF16).astype(F32)
    rest = gains - coarse
    fine = rest.astype(BF16).astype(F32)
    count = jnp.full((2, C), counts[0].astype(F32))
    rows = [coarse, fine, rest - fine, jnp.zeros_like(coarse), count, jnp.zeros((6, C), F32)]
    packed_ref[4 * C :] = jnp.concatenate(rows, 0).astype(BF16)
    for copy in copies:
        copy.wait()


def pair_kernel(chip, x_ref, same, other, outs_ref, skip_ref, rows_same, rows_other, packed, states, pres, sems):
    here, core = position()

    def keep(slot, index, value):
        @pl.when(core == slot)
        def _():
            rows_same[index] = value

        @pl.when(core != slot)
        def _():
            rows_other[index] = value

    @pl.when(here == chip)
    def _():
        weights = Weights(core, [same, other], packed, sems)
        weights.start(0)
        state = (x_ref[core] if chip == FIRST else x_ref[1]).astype(F32)
        for slot in range(2):
            weights.wait(slot)
            weights.forward(slot, state, states, pres, outs_ref)
            keep(slot, 0, outs_ref[slot])
            keep(slot, 1, state.astype(BF16))
            state = outs_ref[slot].astype(F32)
        if chip == SECOND:
            skip_ref[:2] = x_ref[...]
            skip_ref[2:] = outs_ref[...]


def middle_forward_kernel(hop_ref, *refs):
    refs, (outs_ref, inflow_ref, hop_out, state_ref, pre_ref, packed, sems) = refs[:6], refs[6:]
    here, core = position()

    @pl.when(here == MIDDLE)
    def _():
        weights = Weights(core, refs, packed, sems)
        for pair in range(3):
            weights.start(pair)
        for slot in range(6):
            weights.wait(slot)
            state = (hop_ref[...] if slot == 0 else outs_ref[slot - 1]).astype(F32)
            if slot >= 4:
                state = state + outs_ref[7 - slot].astype(F32)
            inflow_ref[slot] = state.astype(BF16)
            weights.forward(slot, state, state_ref, pre_ref, outs_ref)
        hop_out[0] = (outs_ref[5].astype(F32) + outs_ref[1].astype(F32)).astype(BF16)
        hop_out[1] = outs_ref[0]


def store_by_owner(core, slot, refs, index, value):
    left_same, left_other, right_same, right_other, own_other, own_same = refs
    same, other = ((left_same, left_other), (own_same, own_other), (right_same, right_other))[slot // 2]

    @pl.when(core == slot % 2)
    def _():
        same[index] = value

    @pl.when(core != slot % 2)
    def _():
        other[index] = value


def last_kernel(hop_ref, skip_ref, ct_ref, outs_in, inflow_in, *refs):
    refs, refs_out = refs[:6], refs[6:]
    owners, (hop_out, sent_out, up_ref) = refs_out[:6], refs_out[6:9]
    packed, outs_ref, inflow_ref, state_ref, pre_ref, sent_ref, grad_ref, sems = refs_out[9:]
    here, core = position()

    def keep_rows(slots, outs, inflows):
        for slot in slots:
            store_by_owner(core, slot, owners, 0, outs[slot])
            store_by_owner(core, slot, owners, 1, inflows[slot])

    @pl.when(here == LAST)
    def _():
        weights = Weights(core, refs, packed, sems)
        for pair in range(3):
            weights.start(pair)
        skips = [None, hop_ref.at[1]] + [skip_ref.at[index] for index in (3, 2, 1, 0)]
        for slot in range(6):
            weights.wait(slot)
            state = (hop_ref[0] if slot == 0 else outs_ref[slot - 1]).astype(F32)
            if slot:
                state = state + skips[slot][...].astype(F32)
            inflow_ref[slot] = state.astype(BF16)
            weights.forward(slot, state, state_ref, pre_ref, outs_ref)
        for slot in reversed(range(6)):
            up_ref[slot] = ct_ref[core] if slot == 5 else sent_ref[slot + 1]
            grad = up_ref[slot].astype(F32)
            sent_ref[slot] = weights.backward(slot, grad, state_ref, pre_ref, grad_ref)
        hop_out[...] = sent_ref[:2]
        sent_out[...] = sent_ref[2:]
        keep_rows(range(6), outs_ref, inflow_ref)

    @pl.when(here == MIDDLE)
    def _():
        keep_rows(range(6), outs_in, inflow_in)


def middle_backward_kernel(hop_ref, state_ref, pre_ref, x_ref, *refs):
    refs, low_refs, refs_out = refs[:6], refs[6:10], refs[10:]
    hop_out, up_ref, low_state, low_pre, packed, sent_ref, grad_ref, sems = refs_out
    here, core = position()

    @pl.when(here == SECOND)
    def _():
        weights = Weights(core, low_refs, packed, sems)
        for pair in range(2):
            weights.start(pair)
        for slot in range(4):
            weights.wait(slot)
            state = (x_ref[core] if slot == 0 else sent_ref[slot - 1]).astype(F32)
            weights.forward(slot, state, low_state, low_pre, sent_ref)

    @pl.when(here == MIDDLE)
    def _():
        weights = Weights(core, refs, packed, sems)
        for pair in reversed(range(3)):
            weights.start(pair)
        skips = [hop_ref.at[1], hop_ref.at[0], sent_ref.at[5], sent_ref.at[4]]
        for slot in reversed(range(6)):
            weights.wait(slot)
            grad = (hop_ref[0] if slot == 5 else sent_ref[slot + 1]).astype(F32)
            if slot < 4:
                grad = grad + skips[slot][...].astype(F32)
            up_ref[slot] = grad.astype(BF16)
            sent_ref[slot] = weights.backward(slot, grad, state_ref, pre_ref, grad_ref)
        hop_out[...] = sent_ref[0]


def first_backward_kernel(hop_ref, skip_ref, state_ref, pre_ref, up_middle, up_last, *refs):
    rows, refs, refs_out = refs[:6], refs[6:10], refs[10:]
    away, own, (packed, sent_ref, grad_ref, sems, role_sems) = refs_out[:4], refs_out[4:6], refs_out[6:]
    here, core = position()
    owners = list(away) + [ref.at[2] for ref in own]

    def rows_copies(other, same):
        return [
            pltpu.make_async_copy(source, target.at[pl.ds(0, 2)], role_sems.at[number])
            for number, (source, target) in enumerate(zip((other, same), own))
        ]

    for chips, (other, same) in (
        ((here == MIDDLE) | (here == LAST), rows[:2]),
        (here == FIRST, (rows[3], rows[2])),
        (here == SECOND, (rows[5], rows[4])),
    ):

        @pl.when(chips)
        def _():
            for copy in rows_copies(other, same):
                copy.start()

    everything = (slice(None), slice(None))

    @pl.when(here == SECOND)
    def _():
        weights = Weights(core, refs, packed, sems)
        for pair in reversed(range(2)):
            weights.start(pair)
        for slot in reversed(range(4)):
            weights.wait(slot)
            grad = (hop_ref[...] if slot == 3 else sent_ref[slot + 1]).astype(F32)
            grad = grad + skip_ref[3 - slot].astype(F32)
            store_by_owner(core, slot, owners, everything, grad.astype(BF16))
            if slot:
                sent_ref[slot] = weights.backward(slot, grad, state_ref, pre_ref, grad_ref)

    for chip, source in ((MIDDLE, up_middle), (LAST, up_last)):

        @pl.when(here == chip)
        def _():
            for slot in range(6):
                store_by_owner(core, slot, owners, everything, source[slot])

    @pl.when((here <= SECOND) | (here == MIDDLE) | (here == LAST))
    def _():
        for copy in rows_copies(*rows[:2]):
            copy.wait()


def owner_kernel(counts, g_ref, w_in_ref, w_out_ref, *refs):
    pieces, (out_ref, parts_ref, inflow_ref, grad_ref, gw_ref) = refs[:10], refs[10:]
    rows, ups, own = pieces[:4], pieces[4:8], (pieces[9], pieces[8])
    here, core = position()
    pixels = grad_ref.shape[0] // 2
    places = [pl.ds(pl.multiple_of(side * pixels, pixels), pixels) for side in (core, 1 - core)]
    everything = (slice(None), slice(None))

    def take_rows(chips, refs):
        @pl.when(chips)
        def _():
            for ref, side, place in zip(refs, (core, 1 - core), places):
                out_ref[side] = ref[0]
                inflow_ref[place] = ref[1].astype(F32)

    def take_ups(chips, refs, index):
        @pl.when(chips)
        def _():
            for ref, place in zip(refs, places):
                grad_ref[place] = ref[index].astype(F32)

    holds = (here == SECOND) | (here == MIDDLE) | (here == LAST)
    take_rows(holds | (here == FIRST), own)
    take_rows((here == MIDDLE - 1) | (here == LAST - 1), rows[:2])
    take_rows((here == MIDDLE + 1) | (here == LAST + 1), rows[2:])
    take_ups(holds, own, 2)
    take_ups((here == SECOND - 1) | (here == MIDDLE - 1) | (here == LAST - 1), ups[:2], everything)
    take_ups((here == MIDDLE + 1) | (here == LAST + 1), ups[2:], everything)

    inflow = inflow_ref[...]
    after, pre0 = layer_forward(inflow, g_ref[0][None], w_in_ref[0], w_out_ref[0])

    def gradients(layer, state, pre, grad):
        gain = g_ref[layer][None]
        grad_cast = grad.astype(BF16)
        d_act = dot_t(grad_cast, w_out_ref[layer])
        sig = jax.nn.sigmoid(pre)
        act = (pre * sig).astype(BF16)
        d_pre = (d_act * (sig * (1.0 + pre * (1.0 - sig)))).astype(BF16)
        scale = scale_of(state)
        unit = state * scale
        normed = (unit * gain).astype(BF16)
        gw_ref[layer] = dot_rows(normed, d_pre)
        gw_ref[2 + layer] = dot_rows(act, grad_cast)
        return scale, unit, d_pre, gain

    @pl.when(counts[0] > 1)
    def _():
        grad = grad_ref[...]
        pre1 = dot((after * scale_of(after) * g_ref[1][None]).astype(BF16), w_in_ref[1])
        scale, unit, d_pre, gain = gradients(1, after, pre1, grad)
        d_unit = dot_t(d_pre, w_in_ref[1]) * gain
        inner = jnp.mean(d_unit * unit, axis=-1, keepdims=True)
        grad_ref[...] = grad + scale * (d_unit - unit * inner)

    @pl.when(counts[0] <= 1)
    def _():
        gw_ref[1] = jnp.zeros((C, C), F32)
        gw_ref[3] = jnp.zeros((C, C), F32)

    gradients(0, inflow, pre0, grad_ref[...])

    columns, double, _ = parts_ref.shape
    for matrix in range(2):
        both = [gw_ref[2 * matrix + layer].reshape(columns, double // 2, C) for layer in range(2)]
        parts_ref[:, :, matrix * C : (matrix + 1) * C] = jnp.concatenate(both, 1).astype(BF16)


def sum_kernel(parts_ref, w_ref, g_ref, gw_in_ref, gw_out_ref, gain_ref):
    columns, double, _ = parts_ref.shape
    total = parts_ref[0].astype(F32)
    for source in range(1, columns):
        total = total + parts_ref[source].astype(F32)
    share = double // 2
    for layer in range(2):
        rows = total[layer * share : (layer + 1) * share]
        gw_in_ref[layer] = rows[:, :C]
        gw_out_ref[layer] = rows[:, C:]
        product = rows[:, :C] * w_ref[layer]
        ones = jnp.ones((1, C), F32)
        product = lax.dot_general(
            ones, product, (((1,), (1,)), ((), ())), precision=lax.Precision.HIGHEST, preferred_element_type=F32
        )
        gain_ref[layer : layer + 1] = product / g_ref[layer : layer + 1]


def vmem():
    return pl.BlockSpec(memory_space=pltpu.VMEM)


def smem():
    return pl.BlockSpec(memory_space=pltpu.SMEM)


def hbm():
    return pl.BlockSpec(memory_space=pltpu.HBM)


def call(kernel, name, inputs, outputs, scratch=(), us=1, limit=32 * 2**20):
    specs = {"vmem": vmem, "smem": smem, "hbm": hbm}
    outputs = [jax.ShapeDtypeStruct(shape, dtype) for shape, dtype in outputs]
    return pl.pallas_call(
        kernel,
        out_shape=outputs,
        in_specs=[specs[memory]() for memory, _ in inputs],
        out_specs=[vmem() for _ in outputs],
        scratch_shapes=list(scratch),
        compiler_params=pltpu.CompilerParams(vmem_limit_bytes=limit),
        cost_estimate=pl.CostEstimate(flops=us * 10**9, bytes_accessed=2**20, transcendentals=0),
        name=name,
    )(*[array for _, array in inputs])


def at_vmem(*arrays):
    return [("vmem", array) for array in arrays]


def at_hbm(*arrays):
    return [("hbm", array) for array in arrays]


def move(value, chips, cross=False):
    pairs = [(2 * a + core, 2 * b + (1 - core if cross else core)) for a, b in chips for core in range(2)]
    return lax.ppermute(value, "section", pairs)


def packed_scratch(slots):
    return pltpu.VMEM((slots, PACK, C), BF16)


def kept(slots, pixels):
    return pltpu.VMEM((slots, 2, pixels, C), F32)


def body(images, cotangent, w_in, w_out, gains, layer_counts):
    columns = lax.axis_size("dp")
    micro, pixels, _ = images.shape
    tile = (pixels, C)
    dma = pltpu.SemaphoreType.DMA
    barrier = lax.optimization_barrier

    (own,) = call(
        pack_kernel,
        "pack",
        [("smem", layer_counts)] + at_hbm(w_in[0], w_out[0], gains[0]),
        [((PACK, C), BF16)],
        [pltpu.VMEM((2, C), F32), dma((9,))],
        limit=62600000,
    )
    holders = (MIDDLE, LAST)
    low_own = move(own, [(chip, chip) for chip in (FIRST, SECOND)], cross=True)
    left = move(own, [(chip - 1, chip) for chip in holders])
    right = move(own, [(chip + 1, chip) for chip in holders])

    def pair(chip, value):
        return call(
            lambda *refs: pair_kernel(chip, *refs),
            "pair_forward",
            at_vmem(value) + at_hbm(own, low_own),
            [((2,) + tile, BF16), ((4,) + tile, BF16)] + [((2,) + tile, BF16)] * 2,
            [packed_scratch(2), kept(2, pixels), kept(2, pixels), dma((2,))],
        )

    outs_a, _, *rows_a = pair(FIRST, images)
    outs_b, skip, *rows_b = pair(SECOND, move(outs_a, [(FIRST, SECOND)]))
    hop = move(outs_b[1], [(SECOND, MIDDLE)])
    partner = move(barrier((own, low_own))[0], [(chip, chip) for chip in holders], cross=True)
    left, right, later, partner, skip, hop = barrier((left, right, own, partner, skip, hop))
    skip = move(skip, [(SECOND, LAST)])
    left_partner = move(left, [(chip, chip) for chip in holders], cross=True)
    right_partner = move(right, [(chip, chip) for chip in holders], cross=True)
    weights = at_hbm(left, left_partner, own, partner, right, right_partner)
    four, six = (4,) + tile, (6,) + tile
    four_state, six_state = (4, 2) + tile, (6, 2) + tile

    outs, inflows, hop, states, pres = call(
        middle_forward_kernel,
        "middle_forward",
        at_vmem(hop) + weights,
        [(six, BF16), (six, BF16), ((2,) + tile, BF16), (six_state, F32), (six_state, F32)],
        [packed_scratch(6), dma((6,))],
        us=3,
    )
    hop = move(hop, [(MIDDLE, LAST)])
    low_left = move(later, [(SECOND - 1, SECOND)])
    low_partner = move(low_left, [(SECOND, SECOND)], cross=True)
    low_weights = at_hbm(low_left, low_partner, own, low_own)
    *to_owners, hop, skips, ups_last = call(
        last_kernel,
        "last_both",
        at_vmem(hop, skip, cotangent, outs, inflows) + weights,
        [((2,) + tile, BF16)] * 6 + [((2,) + tile, BF16), (four, BF16), (six, BF16)],
        [
            packed_scratch(6),
            pltpu.VMEM(six, BF16),
            pltpu.VMEM(six, BF16),
            kept(6, pixels),
            kept(6, pixels),
            pltpu.VMEM(six, BF16),
            pltpu.VMEM(tile, F32),
            dma((6,)),
        ],
        us=8,
    )
    hop = move(hop, [(LAST, MIDDLE)])
    skips = move(skips, [(LAST, SECOND)])

    def deliver(chips, *pieces):
        lefts = [(chip, chip - 1) for chip in chips]
        rights = [(chip, chip + 1) for chip in (MIDDLE, LAST)]
        routes = ((lefts, False), (lefts, True), (rights, False), (rights, True))
        return [move(piece, *route) for piece, route in zip(pieces, routes) if piece is not None]

    *away, rows_other, rows_same = to_owners
    rows_left, rows_right = away[:2], deliver((MIDDLE, LAST), None, None, *away[2:])
    hop, rows_right = barrier((hop, rows_right))
    hop, ups_middle, low_states, low_pres = call(
        middle_backward_kernel,
        "middle_backward",
        at_vmem(hop, states, pres, images) + weights + low_weights,
        [(tile, BF16), (six, BF16), (four_state, F32), (four_state, F32)],
        [packed_scratch(6), pltpu.VMEM(six, BF16), pltpu.VMEM(tile, F32), dma((6,))],
        us=5,
    )
    rows_left, hop = barrier((rows_left, hop))
    hop = move(hop, [(MIDDLE, SECOND)])
    rows = deliver((MIDDLE, LAST), *rows_left) + rows_right
    *away, own_other, own_same = call(
        first_backward_kernel,
        "first_backward",
        at_vmem(hop, skips, low_states, low_pres, ups_middle, ups_last)
        + at_hbm(rows_other, rows_same, *rows_a, *rows_b)
        + low_weights,
        [(tile, BF16)] * 4 + [((3,) + tile, BF16)] * 2,
        [packed_scratch(4), pltpu.VMEM(four, BF16), pltpu.VMEM(tile, F32), dma((4,)), dma((2,))],
        us=3,
    )
    ups = deliver((SECOND, MIDDLE, LAST), *away)
    own_other = move(own_other, [(chip, chip) for chip in (FIRST, SECOND, MIDDLE, LAST)], cross=True)

    share = C // columns
    section_outputs, parts = call(
        owner_kernel,
        "owner_gradients",
        [("smem", layer_counts)] + at_vmem(gains[0], w_in[0], w_out[0], *rows, *ups, own_other, own_same),
        [((micro, pixels, C), BF16), ((columns, 2 * share, 2 * C), BF16)],
        [pltpu.VMEM((micro * pixels, C), F32)] * 2 + [pltpu.VMEM((4, C, C), F32)],
    )
    parts = lax.all_to_all(parts, "dp", 0, 0, tiled=True)
    start = lax.axis_index("dp") * share
    w_rows = lax.dynamic_slice_in_dim(w_in[0], start, share, 1).astype(F32)
    gain_rows = lax.dynamic_slice_in_dim(gains[0], start, share, 1)
    grad_in, grad_out, grad_gain = call(
        sum_kernel,
        "sum_parts",
        at_vmem(parts, w_rows, gain_rows),
        [((2, share, C), F32), ((2, share, C), F32), ((2, share), F32)],
    )
    return section_outputs[None], grad_in[None], grad_out[None], grad_gain[None]


def solution(mesh):
    return jax.shard_map(
        body,
        mesh=mesh,
        in_specs=(
            P(None, "dp", None),
            P(None, "dp", None),
            P("section", None, None, None),
            P("section", None, None, None),
            P("section", None, None),
            P("section"),
        ),
        out_specs=(
            P("section", None, "dp", None),
            P("section", None, "dp", None),
            P("section", None, "dp", None),
            P("section", None, "dp"),
        ),
        check_vma=False,
    )
```

```python
import functools

import jax
import jax.numpy as jnp
from jax import lax
from jax.experimental import pallas as pl
from jax.experimental.pallas import tpu as pltpu
from jax.sharding import PartitionSpec as P

C = 256
EPS = 1e-06
F32 = jnp.float32
BF16 = jnp.bfloat16
PACK = 4 * C + 16
FIRST, SECOND, MIDDLE, LAST = 0, 1, 3, 6


def dot(a, b):
    return jnp.dot(a, b, preferred_element_type=F32)


def dot_t(a, b):
    return lax.dot_general(a, b, (((1,), (1,)), ((), ())), preferred_element_type=F32)


def dot_rows(a, b):
    return lax.dot_general(a, b, (((0,), (0,)), ((), ())), preferred_element_type=F32)


def scale_of(state):
    return lax.rsqrt(jnp.mean(state * state, axis=-1, keepdims=True) + EPS)


def layer_forward(state, gain, first, second):
    normed = (state * scale_of(state) * gain).astype(BF16)
    pre = dot(normed, first)
    act = (pre * jax.nn.sigmoid(pre)).astype(BF16)
    return state + dot(act, second), pre


def layer_backward(grad, state, pre, gain, first, second):
    d_act = dot_t(grad.astype(BF16), second)
    sig = jax.nn.sigmoid(pre)
    slope = sig * (1.0 + pre * (1.0 - sig))
    d_pre = (d_act * slope).astype(BF16)
    d_normed = dot_t(d_pre, first)
    scale = scale_of(state)
    unit = state * scale
    d_unit = d_normed * gain
    inner = jnp.mean(d_unit * unit, axis=-1, keepdims=True)
    return grad + scale * (d_unit - unit * inner)


def position():
    here = lax.axis_index("section")
    return here // 2, here % 2


class Weights:
    def __init__(self, core, refs, packed, sems):
        self.refs, self.packed, self.sems, self.core = refs, packed, sems, core

    def copy(self, ref, slot):
        return pltpu.make_async_copy(ref, self.packed.at[slot], self.sems.at[slot])

    def start(self, pair):
        same, other = self.refs[2 * pair], self.refs[2 * pair + 1]
        self.copy(same, 2 * pair + self.core).start()
        self.copy(other, 2 * pair + 1 - self.core).start()

    def wait(self, slot):
        self.copy(self.refs[0], slot).wait()

    def tail(self, slot):
        return self.packed[slot, 4 * C :].astype(F32)

    def gain(self, slot, layer):
        tail = self.tail(slot)
        return tail[layer : layer + 1] + tail[2 + layer : 3 + layer] + tail[4 + layer : 5 + layer]

    def first(self, slot, layer):
        return self.packed[slot, layer * C : (layer + 1) * C]

    def second(self, slot, layer):
        return self.packed[slot, (2 + layer) * C : (3 + layer) * C]

    def both(self, slot):
        return jnp.max(self.tail(slot)[8:9]) > 1.5

    def forward(self, slot, state, state_ref, pre_ref, out_ref):
        state_ref[slot, 0] = state
        state, pre = layer_forward(state, self.gain(slot, 0), self.first(slot, 0), self.second(slot, 0))
        pre_ref[slot, 0] = pre
        out_ref[slot] = state.astype(BF16)

        @pl.when(self.both(slot))
        def _():
            state_ref[slot, 1] = state
            after, pre = layer_forward(state, self.gain(slot, 1), self.first(slot, 1), self.second(slot, 1))
            pre_ref[slot, 1] = pre
            out_ref[slot] = after.astype(BF16)

    def backward(self, slot, grad, state_ref, pre_ref, grad_ref):
        grad_ref[...] = grad

        def layer(number):
            return layer_backward(
                grad_ref[...],
                state_ref[slot, number],
                pre_ref[slot, number],
                self.gain(slot, number),
                self.first(slot, number),
                self.second(slot, number),
            )

        @pl.when(self.both(slot))
        def _():
            grad_ref[...] = layer(1)

        return layer(0).astype(BF16)


def pack_kernel(counts, w_in_ref, w_out_ref, g_ref, packed_ref, gains_ref, sems):
    copies = [
        pltpu.make_async_copy(
            ref.at[layer, pl.ds(part * C // 2, C // 2)],
            packed_ref.at[pl.ds((2 * side + layer) * C + part * C // 2, C // 2)],
            sems.at[4 * side + 2 * layer + part],
        )
        for side, ref in enumerate((w_in_ref, w_out_ref))
        for layer in range(2)
        for part in range(2)
    ]
    gains_copy = pltpu.make_async_copy(g_ref, gains_ref, sems.at[8])
    gains_copy.start()
    for copy in copies:
        copy.start()
    gains_copy.wait()
    gains = gains_ref[...]
    coarse = gains.astype(BF16).astype(F32)
    rest = gains - coarse
    fine = rest.astype(BF16).astype(F32)
    count = jnp.full((2, C), counts[0].astype(F32))
    rows = [coarse, fine, rest - fine, jnp.zeros_like(coarse), count, jnp.zeros((6, C), F32)]
    packed_ref[4 * C :] = jnp.concatenate(rows, 0).astype(BF16)
    for copy in copies:
        copy.wait()


def pair_kernel(chip, x_ref, same, other, outs_ref, skip_ref, rows_same, rows_other, packed, states, pres, sems):
    here, core = position()

    def keep(slot, index, value):
        @pl.when(core == slot)
        def _():
            rows_same[index] = value

        @pl.when(core != slot)
        def _():
            rows_other[index] = value

    @pl.when(here == chip)
    def _():
        weights = Weights(core, [same, other], packed, sems)
        weights.start(0)
        state = (x_ref[core] if chip == FIRST else x_ref[1]).astype(F32)
        for slot in range(2):
            weights.wait(slot)
            weights.forward(slot, state, states, pres, outs_ref)
            keep(slot, 0, outs_ref[slot])
            keep(slot, 1, state.astype(BF16))
            state = outs_ref[slot].astype(F32)
        if chip == SECOND:
            skip_ref[:2] = x_ref[...]
            skip_ref[2:] = outs_ref[...]


def middle_forward_kernel(hop_ref, *refs):
    refs, (outs_ref, inflow_ref, hop_out, state_ref, pre_ref, packed, sems) = refs[:6], refs[6:]
    here, core = position()

    @pl.when(here == MIDDLE)
    def _():
        weights = Weights(core, refs, packed, sems)
        for pair in range(3):
            weights.start(pair)
        for slot in range(6):
            weights.wait(slot)
            state = (hop_ref[...] if slot == 0 else outs_ref[slot - 1]).astype(F32)
            if slot >= 4:
                state = state + outs_ref[7 - slot].astype(F32)
            inflow_ref[slot] = state.astype(BF16)
            weights.forward(slot, state, state_ref, pre_ref, outs_ref)
        hop_out[0] = (outs_ref[5].astype(F32) + outs_ref[1].astype(F32)).astype(BF16)
        hop_out[1] = outs_ref[0]


def store_by_owner(core, slot, refs, index, value):
    left_same, left_other, right_same, right_other, own_other, own_same = refs
    same, other = ((left_same, left_other), (own_same, own_other), (right_same, right_other))[slot // 2]

    @pl.when(core == slot % 2)
    def _():
        same[index] = value

    @pl.when(core != slot % 2)
    def _():
        other[index] = value


def last_kernel(hop_ref, skip_ref, ct_ref, outs_in, inflow_in, *refs):
    refs, refs_out = refs[:6], refs[6:]
    owners, (hop_out, sent_out, up_ref) = refs_out[:6], refs_out[6:9]
    packed, outs_ref, inflow_ref, state_ref, pre_ref, sent_ref, grad_ref, sems = refs_out[9:]
    here, core = position()

    def keep_rows(slots, outs, inflows):
        for slot in slots:
            store_by_owner(core, slot, owners, 0, outs[slot])
            store_by_owner(core, slot, owners, 1, inflows[slot])

    @pl.when(here == LAST)
    def _():
        weights = Weights(core, refs, packed, sems)
        for pair in range(3):
            weights.start(pair)
        skips = [None, hop_ref.at[1]] + [skip_ref.at[index] for index in (3, 2, 1, 0)]
        for slot in range(6):
            weights.wait(slot)
            state = (hop_ref[0] if slot == 0 else outs_ref[slot - 1]).astype(F32)
            if slot:
                state = state + skips[slot][...].astype(F32)
            store_by_owner(core, slot, owners, 1, state.astype(BF16))
            weights.forward(slot, state, state_ref, pre_ref, outs_ref)
        sent = [hop_out.at[0], hop_out.at[1]] + [sent_out.at[index] for index in range(4)]
        for slot in reversed(range(6)):
            up_ref[slot] = ct_ref[core] if slot == 5 else sent[slot + 1][...]
            grad = up_ref[slot].astype(F32)
            sent[slot][...] = weights.backward(slot, grad, state_ref, pre_ref, grad_ref)
        for slot in range(6):
            store_by_owner(core, slot, owners, 0, outs_ref[slot])

    @pl.when(here == MIDDLE)
    def _():
        keep_rows(range(6), outs_in, inflow_in)


def middle_backward_kernel(hop_ref, state_ref, pre_ref, x_ref, *refs):
    refs, low_refs, refs_out = refs[:6], refs[6:10], refs[10:]
    hop_out, up_ref, low_state, low_pre, packed, sent_ref, grad_ref, sems = refs_out
    here, core = position()

    @pl.when(here == SECOND)
    def _():
        weights = Weights(core, low_refs, packed, sems)
        for pair in range(2):
            weights.start(pair)
        for slot in range(4):
            weights.wait(slot)
            state = (x_ref[core] if slot == 0 else sent_ref[slot - 1]).astype(F32)
            weights.forward(slot, state, low_state, low_pre, sent_ref)

    @pl.when(here == MIDDLE)
    def _():
        weights = Weights(core, refs, packed, sems)
        for pair in reversed(range(3)):
            weights.start(pair)
        skips = [hop_ref.at[1], hop_ref.at[0], sent_ref.at[5], sent_ref.at[4]]
        for slot in reversed(range(6)):
            weights.wait(slot)
            grad = (hop_ref[0] if slot == 5 else sent_ref[slot + 1]).astype(F32)
            if slot < 4:
                grad = grad + skips[slot][...].astype(F32)
            up_ref[slot] = grad.astype(BF16)
            sent_ref[slot] = weights.backward(slot, grad, state_ref, pre_ref, grad_ref)
        hop_out[...] = sent_ref[0]


def first_backward_kernel(hop_ref, skip_ref, state_ref, pre_ref, up_middle, up_last, *refs):
    rows, refs, refs_out = refs[:6], refs[6:10], refs[10:]
    away, own, (packed, sent_ref, grad_ref, sems, role_sems) = refs_out[:4], refs_out[4:6], refs_out[6:]
    here, core = position()
    owners = list(away) + [ref.at[2] for ref in own]

    def rows_copies(other, same):
        return [
            pltpu.make_async_copy(source, target.at[pl.ds(0, 2)], role_sems.at[number])
            for number, (source, target) in enumerate(zip((other, same), own))
        ]

    for chips, (other, same) in (
        ((here == MIDDLE) | (here == LAST), rows[:2]),
        (here == FIRST, (rows[3], rows[2])),
        (here == SECOND, (rows[5], rows[4])),
    ):

        @pl.when(chips)
        def _():
            for copy in rows_copies(other, same):
                copy.start()

    everything = (slice(None), slice(None))

    @pl.when(here == SECOND)
    def _():
        weights = Weights(core, refs, packed, sems)
        for pair in reversed(range(2)):
            weights.start(pair)
        for slot in reversed(range(4)):
            weights.wait(slot)
            grad = (hop_ref[...] if slot == 3 else sent_ref[slot + 1]).astype(F32)
            grad = grad + skip_ref[3 - slot].astype(F32)
            store_by_owner(core, slot, owners, everything, grad.astype(BF16))
            if slot:
                sent_ref[slot] = weights.backward(slot, grad, state_ref, pre_ref, grad_ref)

    for chip, source in ((MIDDLE, up_middle), (LAST, up_last)):

        @pl.when(here == chip)
        def _():
            for slot in range(6):
                store_by_owner(core, slot, owners, everything, source[slot])

    @pl.when((here <= SECOND) | (here == MIDDLE) | (here == LAST))
    def _():
        for copy in rows_copies(*rows[:2]):
            copy.wait()


def owner_kernel(counts, g_ref, w_in_ref, w_out_ref, *refs):
    pieces, (out_ref, parts_ref, inflow_ref, grad_ref, gw_ref) = refs[:10], refs[10:]
    rows, ups, own = pieces[:4], pieces[4:8], (pieces[9], pieces[8])
    here, core = position()
    pixels = grad_ref.shape[0] // 2
    places = [pl.ds(pl.multiple_of(side * pixels, pixels), pixels) for side in (core, 1 - core)]
    everything = (slice(None), slice(None))

    def take_rows(chips, refs):
        @pl.when(chips)
        def _():
            for ref, side, place in zip(refs, (core, 1 - core), places):
                out_ref[side] = ref[0]
                inflow_ref[place] = ref[1].astype(F32)

    def take_ups(chips, refs, index):
        @pl.when(chips)
        def _():
            for ref, place in zip(refs, places):
                grad_ref[place] = ref[index].astype(F32)

    holds = (here == SECOND) | (here == MIDDLE) | (here == LAST)
    take_rows(holds | (here == FIRST), own)
    take_rows((here == MIDDLE - 1) | (here == LAST - 1), rows[:2])
    take_rows((here == MIDDLE + 1) | (here == LAST + 1), rows[2:])
    take_ups(holds, own, 2)
    take_ups((here == SECOND - 1) | (here == MIDDLE - 1) | (here == LAST - 1), ups[:2], everything)
    take_ups((here == MIDDLE + 1) | (here == LAST + 1), ups[2:], everything)

    inflow = inflow_ref[...]
    after, pre0 = layer_forward(inflow, g_ref[0][None], w_in_ref[0], w_out_ref[0])

    def gradients(layer, state, pre, grad):
        gain = g_ref[layer][None]
        grad_cast = grad.astype(BF16)
        d_act = dot_t(grad_cast, w_out_ref[layer])
        sig = jax.nn.sigmoid(pre)
        act = (pre * sig).astype(BF16)
        d_pre = (d_act * (sig * (1.0 + pre * (1.0 - sig)))).astype(BF16)
        scale = scale_of(state)
        unit = state * scale
        normed = (unit * gain).astype(BF16)
        gw_ref[layer] = dot_rows(normed, d_pre)
        gw_ref[2 + layer] = dot_rows(act, grad_cast)
        return scale, unit, d_pre, gain

    @pl.when(counts[0] > 1)
    def _():
        grad = grad_ref[...]
        pre1 = dot((after * scale_of(after) * g_ref[1][None]).astype(BF16), w_in_ref[1])
        scale, unit, d_pre, gain = gradients(1, after, pre1, grad)
        d_unit = dot_t(d_pre, w_in_ref[1]) * gain
        inner = jnp.mean(d_unit * unit, axis=-1, keepdims=True)
        grad_ref[...] = grad + scale * (d_unit - unit * inner)

    @pl.when(counts[0] <= 1)
    def _():
        gw_ref[1] = jnp.zeros((C, C), F32)
        gw_ref[3] = jnp.zeros((C, C), F32)

    gradients(0, inflow, pre0, grad_ref[...])

    columns, double, _ = parts_ref.shape
    for matrix in range(2):
        both = [gw_ref[2 * matrix + layer].reshape(columns, double // 2, C) for layer in range(2)]
        parts_ref[:, :, matrix * C : (matrix + 1) * C] = jnp.concatenate(both, 1).astype(BF16)


def sum_kernel(parts_ref, w_ref, g_ref, gw_in_ref, gw_out_ref, gain_ref):
    columns, double, _ = parts_ref.shape
    total = parts_ref[0].astype(F32)
    for source in range(1, columns):
        total = total + parts_ref[source].astype(F32)
    share = double // 2
    for layer in range(2):
        rows = total[layer * share : (layer + 1) * share]
        gw_in_ref[layer] = rows[:, :C]
        gw_out_ref[layer] = rows[:, C:]
        product = rows[:, :C] * w_ref[layer]
        ones = jnp.ones((1, C), F32)
        product = lax.dot_general(
            ones, product, (((1,), (1,)), ((), ())), precision=lax.Precision.HIGHEST, preferred_element_type=F32
        )
        gain_ref[layer : layer + 1] = product / g_ref[layer : layer + 1]


def vmem():
    return pl.BlockSpec(memory_space=pltpu.VMEM)


def smem():
    return pl.BlockSpec(memory_space=pltpu.SMEM)


def hbm():
    return pl.BlockSpec(memory_space=pltpu.HBM)


def call(kernel, name, inputs, outputs, scratch=(), us=1, limit=32 * 2**20):
    specs = {"vmem": vmem, "smem": smem, "hbm": hbm}
    outputs = [jax.ShapeDtypeStruct(shape, dtype) for shape, dtype in outputs]
    return pl.pallas_call(
        kernel,
        out_shape=outputs,
        in_specs=[specs[memory]() for memory, _ in inputs],
        out_specs=[vmem() for _ in outputs],
        scratch_shapes=list(scratch),
        compiler_params=pltpu.CompilerParams(vmem_limit_bytes=limit),
        cost_estimate=pl.CostEstimate(flops=us * 10**9, bytes_accessed=2**20, transcendentals=0),
        name=name,
    )(*[array for _, array in inputs])


def at_vmem(*arrays):
    return [("vmem", array) for array in arrays]


def at_hbm(*arrays):
    return [("hbm", array) for array in arrays]


def move(value, chips, cross=False):
    pairs = [(2 * a + core, 2 * b + (1 - core if cross else core)) for a, b in chips for core in range(2)]
    return lax.ppermute(value, "section", pairs)


def packed_scratch(slots):
    return pltpu.VMEM((slots, PACK, C), BF16)


def kept(slots, pixels):
    return pltpu.VMEM((slots, 2, pixels, C), F32)


def body(images, cotangent, w_in, w_out, gains, layer_counts):
    columns = lax.axis_size("dp")
    micro, pixels, _ = images.shape
    tile = (pixels, C)
    dma = pltpu.SemaphoreType.DMA
    barrier = lax.optimization_barrier

    (own,) = call(
        pack_kernel,
        "pack",
        [("smem", layer_counts)] + at_hbm(w_in[0], w_out[0], gains[0]),
        [((PACK, C), BF16)],
        [pltpu.VMEM((2, C), F32), dma((9,))],
        limit=62600000,
    )
    holders = (MIDDLE, LAST)
    low_own = move(own, [(chip, chip) for chip in (FIRST, SECOND)], cross=True)
    left = move(own, [(chip - 1, chip) for chip in holders])
    right = move(own, [(chip + 1, chip) for chip in holders])

    def pair(chip, value):
        return call(
            lambda *refs: pair_kernel(chip, *refs),
            "pair_forward",
            at_vmem(value) + at_hbm(own, low_own),
            [((2,) + tile, BF16), ((4,) + tile, BF16)] + [((2,) + tile, BF16)] * 2,
            [packed_scratch(2), kept(2, pixels), kept(2, pixels), dma((2,))],
        )

    outs_a, _, *rows_a = pair(FIRST, images)
    outs_b, skip, *rows_b = pair(SECOND, move(outs_a, [(FIRST, SECOND)]))
    hop = move(outs_b[1], [(SECOND, MIDDLE)])
    partner = move(barrier((own, low_own))[0], [(chip, chip) for chip in holders], cross=True)
    left, right, later, partner, skip, hop = barrier((left, right, own, partner, skip, hop))
    skip = move(skip, [(SECOND, LAST)])
    left_partner = move(left, [(chip, chip) for chip in holders], cross=True)
    right_partner = move(right, [(chip, chip) for chip in holders], cross=True)
    weights = at_hbm(left, left_partner, own, partner, right, right_partner)
    four, six = (4,) + tile, (6,) + tile
    four_state, six_state = (4, 2) + tile, (6, 2) + tile

    outs, inflows, hop, states, pres = call(
        middle_forward_kernel,
        "middle_forward",
        at_vmem(hop) + weights,
        [(six, BF16), (six, BF16), ((2,) + tile, BF16), (six_state, F32), (six_state, F32)],
        [packed_scratch(6), dma((6,))],
        us=3,
    )
    hop = move(hop, [(MIDDLE, LAST)])
    low_left = move(later, [(SECOND - 1, SECOND)])
    low_partner = move(low_left, [(SECOND, SECOND)], cross=True)
    low_weights = at_hbm(low_left, low_partner, own, low_own)
    *to_owners, hop, skips, ups_last = call(
        last_kernel,
        "last_both",
        at_vmem(hop, skip, cotangent, outs, inflows) + weights,
        [((2,) + tile, BF16)] * 6 + [((2,) + tile, BF16), (four, BF16), (six, BF16)],
        [
            packed_scratch(6),
            pltpu.VMEM(six, BF16),
            pltpu.VMEM(six, BF16),
            kept(6, pixels),
            kept(6, pixels),
            pltpu.VMEM(six, BF16),
            pltpu.VMEM(tile, F32),
            dma((6,)),
        ],
        us=8,
    )
    hop = move(hop, [(LAST, MIDDLE)])
    skips = move(skips, [(LAST, SECOND)])

    def deliver(chips, *pieces):
        lefts = [(chip, chip - 1) for chip in chips]
        rights = [(chip, chip + 1) for chip in (MIDDLE, LAST)]
        routes = ((lefts, False), (lefts, True), (rights, False), (rights, True))
        return [move(piece, *route) for piece, route in zip(pieces, routes) if piece is not None]

    *away, rows_other, rows_same = to_owners
    rows_left, rows_right = away[:2], deliver((MIDDLE, LAST), None, None, *away[2:])
    hop, rows_right = barrier((hop, rows_right))
    hop, ups_middle, low_states, low_pres = call(
        middle_backward_kernel,
        "middle_backward",
        at_vmem(hop, states, pres, images) + weights + low_weights,
        [(tile, BF16), (six, BF16), (four_state, F32), (four_state, F32)],
        [packed_scratch(6), pltpu.VMEM(six, BF16), pltpu.VMEM(tile, F32), dma((6,))],
        us=5,
    )
    rows_left, hop = barrier((rows_left, hop))
    hop = move(hop, [(MIDDLE, SECOND)])
    rows = deliver((MIDDLE, LAST), *rows_left) + rows_right
    *away, own_other, own_same = call(
        first_backward_kernel,
        "first_backward",
        at_vmem(hop, skips, low_states, low_pres, ups_middle, ups_last)
        + at_hbm(rows_other, rows_same, *rows_a, *rows_b)
        + low_weights,
        [(tile, BF16)] * 4 + [((3,) + tile, BF16)] * 2,
        [packed_scratch(4), pltpu.VMEM(four, BF16), pltpu.VMEM(tile, F32), dma((4,)), dma((2,))],
        us=3,
    )
    ups = deliver((SECOND, MIDDLE, LAST), *away)
    own_other = move(own_other, [(chip, chip) for chip in (FIRST, SECOND, MIDDLE, LAST)], cross=True)

    share = C // columns
    section_outputs, parts = call(
        owner_kernel,
        "owner_gradients",
        [("smem", layer_counts)] + at_vmem(gains[0], w_in[0], w_out[0], *rows, *ups, own_other, own_same),
        [((micro, pixels, C), BF16), ((columns, 2 * share, 2 * C), BF16)],
        [pltpu.VMEM((micro * pixels, C), F32)] * 2 + [pltpu.VMEM((4, C, C), F32)],
    )
    parts = lax.all_to_all(parts, "dp", 0, 0, tiled=True)
    start = lax.axis_index("dp") * share
    w_rows = lax.dynamic_slice_in_dim(w_in[0], start, share, 1).astype(F32)
    gain_rows = lax.dynamic_slice_in_dim(gains[0], start, share, 1)
    grad_in, grad_out, grad_gain = call(
        sum_kernel,
        "sum_parts",
        at_vmem(parts, w_rows, gain_rows),
        [((2, share, C), F32), ((2, share, C), F32), ((2, share), F32)],
    )
    return section_outputs[None], grad_in[None], grad_out[None], grad_gain[None]


def solution(mesh):
    return jax.shard_map(
        body,
        mesh=mesh,
        in_specs=(
            P(None, "dp", None),
            P(None, "dp", None),
            P("section", None, None, None),
            P("section", None, None, None),
            P("section", None, None),
            P("section"),
        ),
        out_specs=(
            P("section", None, "dp", None),
            P("section", None, "dp", None),
            P("section", None, "dp", None),
            P("section", None, "dp"),
        ),
        check_vma=False,
    )
```
